256 devices in a mesh: dp: 16 (over z, x_lo), tensor: 16 (over y, x_hi, core).
Axes of the slice: x: 4 (x_hi: 2, x_lo: 2; x = x_hi * 2 + x_lo), y: 4, z: 8, core: 2. Of those that a mesh axis runs over, the one named last changes fastest.
Arguments:
- gate_act: bfloat16 [2048, 26624], P('dp', 'tensor'), may hold values from -8 to 8
- up_act: bfloat16 [2048, 26624], P('dp', 'tensor'), may hold values from -6 to 6
- down_codes: bfloat16 [26624, 16384], P('tensor', 'dp'), may hold values from -4 to 4
- down_scales: float32 [208, 128], P('tensor', 'dp'), may hold values from 0.0024514517 to 0.024514517
- grad_out: bfloat16 [2048, 16384], P('tensor', 'dp'), may hold values from -6 to 6
Outputs:
- layer_output: bfloat16 [2048, 16384], P('tensor', 'dp')
- gate_grad: bfloat16 [2048, 26624], P('dp', 'tensor')
- up_grad: bfloat16 [2048, 26624], P('dp', 'tensor')
The draws below stay inside these ranges and needn't reach their ends.
All inputs are finite; a program needn't handle non-finite values.
Results may differ from the reference program's by a relative error of at most 0.027.
Values may be sent and summed in bfloat16 or wider, within the bound.
A program may use at most 128 MiB of HBM per device.

```python
import math
import jax
import jax.numpy as jnp
from jax import lax

D = 16384
FF = 26624
BLOCK = 128
TOKENS = 2048
FL = 1664
DL = 1024


def raised(result, stream_key, source, target, blocks, factor):
    owner, partner = [(jnp.arange(result.shape[position]) // (result.shape[position] // blocks)).reshape([-1 if axis == position else 1 for axis in range(result.ndim)]) for position in (source, target)]
    chosen = jax.random.permutation(stream_key, blocks)[partner]
    strong = (owner == chosen) | (owner == (partner + blocks // 2) % blocks)
    return jnp.where(strong, factor * result, result)


def steps_of(own_key, shape, cuts, least, high):
    def one(position, blocks):
        heights = jax.random.uniform(jax.random.fold_in(jax.random.fold_in(own_key, 6), position), (blocks,), jnp.float32, least / len(cuts), high / len(cuts))
        return jnp.repeat(jnp.exp(heights), shape[position] // blocks).reshape((-1,) + (1,) * (len(shape) - position - 1))

    level = one(*cuts[0])
    for cut in cuts[1:]:
        level = level * one(*cut)
    return level


def gaussian(stream_key, shape, deviation, limit, cuts=(), kind=jnp.bfloat16):
    values = deviation * jax.random.normal(stream_key, shape, jnp.float32)
    if cuts:
        values = values * steps_of(stream_key, shape, cuts, -0.22, 0.18)
    return jnp.clip(values, -limit, limit).astype(kind)


def noise_with(rng, dims, deviation, most, pieces, heavy, kind=jnp.bfloat16):
    result = deviation * jax.random.normal(rng, dims, jnp.float32)
    if pieces:
        result = result * steps_of(rng, dims, pieces, -0.22, 0.18)
    return jnp.clip(raised(result, jax.random.fold_in(rng, 3), *heavy), -most, most).astype(kind)


def setup_inputs(seed: int = 0) -> dict:
    splits = jax.random.split(jax.random.key(seed), 6)
    return {
        "gate_act": gaussian(splits[0], (TOKENS, FF), 2.0, 8.0, ((0, 16), (1, 16))),
        "up_act": gaussian(splits[1], (TOKENS, FF), 1.0, 6.0, ((0, 16), (1, 16))),
        "down_codes": gaussian(splits[2], (FF, D), 1.0, 4.0, ((0, 16), (1, 16))),
        "down_scales": jnp.clip(jnp.exp(math.log(0.024514517) - 2.3025851 * jax.random.uniform(splits[3], (FF // BLOCK, D // BLOCK), jnp.float32) ** steps_of(splits[3], (FF // BLOCK, D // BLOCK), ((0, 16), (1, 16)), -0.2, 0.2)), 0.0024514517, 0.024514517),
        "grad_out": noise_with(splits[4], (TOKENS, D), 1.0, 6.0, ((0, 16), (1, 16)), (1, 0, 16, 2.0)),
    }


def sylvester(matrix_order):
    indices = jnp.arange(matrix_order, dtype=jnp.int32)
    common_bits = indices[:, None] & indices[None, :]
    parity = jnp.zeros((matrix_order, matrix_order), jnp.int32)
    for section_bit in range(max(matrix_order.bit_length() - 1, 0)):
        parity = parity + (common_bits >> section_bit & 1)
    return (1 - 2 * (parity % 2)).astype(jnp.float32)

def dequantize(code_block, scale_block):
    row_count, col_count = code_block.shape
    expanded = code_block.astype(jnp.float32).reshape(row_count // BLOCK, BLOCK, col_count // BLOCK, BLOCK)
    return (expanded * scale_block[:, None, :, None]).reshape(row_count, col_count).astype(jnp.bfloat16)

def rotate(values):
    row_count = values.shape[0]
    groups = FF // FL
    shaped = values.astype(jnp.float32).reshape(row_count, groups, FL // BLOCK, BLOCK)
    mixed_values = jnp.einsum('rgbc,hg,dc->rhbd', shaped, sylvester(groups), sylvester(BLOCK), precision=lax.Precision.HIGHEST)
    return (mixed_values / math.sqrt(groups * BLOCK)).reshape(row_count, FF).astype(jnp.bfloat16)

def reference(gate_act, up_act, down_codes, down_scales, grad_out):
    gate_wide = gate_act.astype(jnp.float32)
    up_wide = up_act.astype(jnp.float32)
    sigmoid_gate = jax.nn.sigmoid(gate_wide)
    silu_gate = gate_wide * sigmoid_gate
    hidden = (silu_gate * up_wide).astype(jnp.bfloat16)
    rotated = rotate(hidden)
    groups = FF // FL
    rot_groups = jnp.moveaxis(rotated.reshape(TOKENS, groups, FL), 1, 0)
    code_groups = down_codes.reshape(groups, FL, D)
    scale_groups = down_scales.reshape(groups, FL // BLOCK, D // BLOCK)

    def forward_step(running, inputs):
        rot_part, code_part, scale_part = inputs
        group_term = jnp.dot(rot_part, dequantize(code_part, scale_part), preferred_element_type=jnp.float32)
        group_term = lax.optimization_barrier(group_term.astype(jnp.bfloat16))
        return (running + group_term.astype(jnp.float32), None)
    running, unused = lax.scan(forward_step, jnp.zeros((TOKENS, D), jnp.float32), (rot_groups, code_groups, scale_groups))
    layer_output = running.astype(jnp.bfloat16)
    col_groups = D // DL
    grad_groups = jnp.moveaxis(grad_out.reshape(TOKENS, col_groups, DL), 1, 0)
    code_cols = jnp.moveaxis(down_codes.reshape(FF, col_groups, DL), 1, 0)
    scale_cols = jnp.moveaxis(down_scales.reshape(FF // BLOCK, col_groups, DL // BLOCK), 1, 0)

    def backward_step(running, inputs):
        grad_part, code_part, scale_part = inputs
        weight = dequantize(code_part, scale_part)
        group_term = lax.dot_general(grad_part, weight, (((1,), (1,)), ((), ())), preferred_element_type=jnp.float32)
        group_term = lax.optimization_barrier(group_term.astype(jnp.bfloat16))
        return (running + group_term.astype(jnp.float32), None)
    running, unused = lax.scan(backward_step, jnp.zeros((TOKENS, FF), jnp.float32), (grad_groups, code_cols, scale_cols))
    grad_rotated = running.astype(jnp.bfloat16)
    grad_hidden = rotate(grad_rotated).astype(jnp.float32)
    up_grad = (grad_hidden * silu_gate).astype(jnp.bfloat16)
    gate_grad = (grad_hidden * up_wide * sigmoid_gate * (1.0 + gate_wide * (1.0 - sigmoid_gate))).astype(jnp.bfloat16)
    return (layer_output, gate_grad, up_grad)
```

```python
import math

import jax
import jax.numpy as jnp
import numpy as np
from jax import lax
from jax.experimental import pallas as pl
from jax.experimental.pallas import tpu as pltpu
from jax.sharding import PartitionSpec as P

MESH = pl.DeviceIdType.MESH
F32, BF16 = jnp.float32, jnp.bfloat16
B = 128
FL, DL = 1664, 1024
NZ, NT = 8, 16
HALF = 896
WIDTHS = (896, 768)
ROWS = NZ * B
CHUNKS = tuple((k * 256, min(256, FL - k * 256)) for k in range(7))


def dot(a, b):
    return jnp.dot(a, b, preferred_element_type=F32)


def dot_t(a, b):
    return lax.dot_general(a, b, (((1,), (1,)), ((), ())), preferred_element_type=F32)


def block_rows(index, size=B):
    return pl.ds(pl.multiple_of(index * size, size), size)


def kernel(
    gate_ref, up_ref, codes_ref, scales_ref, grad_ref, had_ref,
    out_ref, gate_grad_ref, up_grad_ref,
    codes_v, w_all, hid, mix_in, mix_out, acts, grads,
    cpart, crecv, csum, yrecv, xsend, xrecv, osend, oacc,
    back, ring, rot_grad, grad_hid,
    code_sem, w_s, w_r, a_s, a_r, ag_s, ag_r,
    gd_s, gd_r, gx_s, gx_r, gy_s, gy_r, gc_s, gc_r,
    c_s, c_r, y_s, y_r, x_s, x_r, o_s, o_r, rs_s, rs_r,
):
    d, t = lax.axis_index("dp"), lax.axis_index("tensor")
    z, xl = lax.div(d, 2), lax.rem(d, 2)
    y, xh, core = lax.div(t, 4), lax.rem(lax.div(t, 2), 2), lax.rem(t, 2)

    def dev(z_=z, xl_=xl, y_=y, xh_=xh, c_=core):
        return (z_ * 2 + xl_, y_ * 4 + xh_ * 2 + c_)

    def zmod(v):
        return lax.rem(v + NZ, NZ)

    partner = dev(xl_=1 - xl)
    diagonal = dev(xl_=1 - xl, c_=1 - core)
    sibling = dev(c_=1 - core)
    across = dev(xh_=1 - xh)
    z_next = (dev(z_=zmod(z + 1)), dev(z_=zmod(z - 1)))
    y_peer = [dev(y_=lax.rem(y + r, 4)) for r in range(4)]
    sent = []

    def copy(src, dst, send, recv, device):
        return pltpu.make_async_remote_copy(
            src_ref=src, dst_ref=dst, send_sem=send, recv_sem=recv, device_id=device, device_id_type=MESH
        )

    def push(*args):
        op = copy(*args)
        op.start()
        sent.append(op)

    def arrived(dst, send, recv):
        copy(dst, dst, send, recv, sibling).wait_recv()

    fetch = pltpu.make_async_copy(codes_ref, codes_v, code_sem)
    fetch.start()

    barrier = pltpu.get_barrier_semaphore()

    def greet(j, carry):
        pl.semaphore_signal(barrier, inc=1, device_id=(d, lax.rem(t + j, NT)), device_id_type=MESH)
        return carry

    lax.fori_loop(1, NT, greet, 0)
    for device in (*z_next, partner, diagonal):
        pl.semaphore_signal(barrier, inc=1, device_id=device, device_id_type=MESH)

    def hidden_rows(i, carry):
        rows = block_rows(i, 16)
        gate = gate_ref[rows, :].astype(F32)
        value = (gate * jax.nn.sigmoid(gate) * up_ref[rows, :].astype(F32)).astype(BF16)
        hid[0, rows, :] = value[:, :HALF]
        hid[1, rows, : WIDTHS[1]] = value[:, HALF:]
        hid[1, rows, WIDTHS[1] :] = jnp.zeros((16, HALF - WIDTHS[1]), BF16)
        rot_grad[1, rows, WIDTHS[1] :] = jnp.zeros((16, HALF - WIDTHS[1]), BF16)
        return carry

    lax.fori_loop(0, 8, hidden_rows, 0)
    pl.semaphore_wait(barrier, NT - 1 + 4)

    def out_copy(i, src, j):
        p = lax.rem(t + j, NT)
        piece = src.at[lax.rem(p, 2), block_rows(lax.div(p, 2), 16), :]
        return copy(piece, mix_in.at[i, t], a_s.at[2 * i, j], a_r.at[2 * i, j], (d, p))

    def scatter(i, src):
        def step(j, carry):
            out_copy(i, src, j).start()
            return carry

        lax.fori_loop(1, NT, step, 0)
        mix_in[i, t] = src[core, block_rows(lax.div(t, 2), 16), :]

    def scattered(i):
        def step(j, carry):
            p = lax.rem(t - j + NT, NT)
            arrived(mix_in.at[i, p], a_s.at[2 * i, j], a_r.at[2 * i, j])
            return carry

        lax.fori_loop(1, NT, step, 0)

    def mix(i):
        had = had_ref[...]
        for b in range(HALF // B):
            cols = slice(b * B, (b + 1) * B)
            mixed = dot(mix_in[i, :, :, cols].reshape(256, B), had)
            parts = [mixed[g * 16 : (g + 1) * 16] for g in range(NT)]
            for bit in (1, 2, 4, 8):
                parts = [parts[g] + parts[g ^ bit] if not g & bit else parts[g ^ bit] - parts[g] for g in range(NT)]
            for g in range(NT):
                mix_out[i, g, :, cols] = (parts[g] * (1.0 / math.sqrt(NT * B))).astype(BF16)

    def back_copy(i, dst, base, j):
        p = lax.rem(t + j, NT)
        landing = dst.at[core, block_rows(base + lax.div(t, 2), 16), :]
        return copy(mix_out.at[i, p], landing, a_s.at[2 * i + 1, j], a_r.at[2 * i + 1, j], (d, p))

    def gather(i, dst, base):
        def step(j, carry):
            back_copy(i, dst, base, j).start()
            return carry

        lax.fori_loop(1, NT, step, 0)
        dst[core, block_rows(base + lax.div(t, 2), 16), :] = mix_out[i, t]

    def gathered(i, dst, base):
        def step(j, carry):
            p = lax.rem(t - j + NT, NT)
            landing = dst.at[lax.rem(p, 2), block_rows(base + lax.div(p, 2), 16), :]
            arrived(landing, a_s.at[2 * i + 1, j], a_r.at[2 * i + 1, j])
            return carry

        lax.fori_loop(1, NT, step, 0)

    scatter(0, hid)

    own_rows, across_rows = block_rows(2 * y + xh), block_rows(2 * y + 1 - xh)
    diagonal_copy = copy(grad_ref, grads.at[xl, own_rows, :], gd_s, gd_r, diagonal)

    @pl.when(core != xl)
    def _():
        diagonal_copy.start()

    @pl.when(core == xl)
    def _():
        grads[core, own_rows, :] = grad_ref[...]

    fetch.wait()

    def weight_copy(k):
        start, size = CHUNKS[k]
        piece = w_all.at[xl, pl.ds(start, size), :]
        return (piece, piece, w_s.at[k], w_r.at[k], partner)

    def weight_arrived(k):
        start, size = CHUNKS[k]
        arrived(w_all.at[1 - xl, pl.ds(start, size), :], w_s.at[k], w_r.at[k])

    def dequantize(k):
        start, size = CHUNKS[k]

        def one(i, carry):
            rows = block_rows(i)
            for j in range(DL // B):
                cols = slice(j * B, (j + 1) * B)
                w_all[xl, rows, cols] = (codes_v[rows, cols].astype(F32) * scales_ref[i, j]).astype(BF16)
            return carry

        lax.fori_loop(start // B, (start + size) // B, one, 0)

    for k in range(len(CHUNKS)):
        dequantize(k)
        push(*weight_copy(k))

    def grad_own():
        @pl.when(core != xl)
        def _():
            arrived(grads.at[core, own_rows, :], gd_s, gd_r)

        mine = grads.at[core, own_rows, :]
        push(mine, mine, gx_s, gx_r, across)
        for r in (1, 3, 2):
            push(mine, mine, gy_s.at[0, r], gy_r.at[0, r], y_peer[r])
        push(mine, mine, gc_s.at[0, 0], gc_r.at[0, 0], sibling)

    def grad_across():
        piece = grads.at[core, across_rows, :]
        arrived(piece, gx_s, gx_r)
        for r in (1, 3, 2):
            push(piece, piece, gy_s.at[1, r], gy_r.at[1, r], y_peer[r])
        push(piece, piece, gc_s.at[1, 0], gc_r.at[1, 0], sibling)

    def grad_y(f, r):
        source = lax.rem(y - r + 4, 4)
        piece = grads.at[core, block_rows(2 * source + (1 - xh if f else xh)), :]
        arrived(piece, gy_s.at[f, r], gy_r.at[f, r])
        push(piece, piece, gc_s.at[f, r], gc_r.at[f, r], sibling)

    def grad_done():
        for f in range(2):
            for r in range(4):
                source = lax.rem(y - r + 4, 4)
                piece = grads.at[1 - core, block_rows(2 * source + (1 - xh if f else xh)), :]
                arrived(piece, gc_s.at[f, r], gc_r.at[f, r])

    def ag_copy(way, s, group):
        block = zmod(z - s) if way == 0 else zmod(z + s)
        piece = acts.at[group, block_rows(block), pl.ds(0, WIDTHS[group])]
        return (piece, piece, ag_s.at[way, s, group], ag_r.at[way, s, group], z_next[way])

    def ag_step(s):
        for way in range(2):
            for group in range(2):
                if s and (s < 4 or way == group):
                    block = zmod(z - s) if way == 0 else zmod(z + s)
                    piece = acts.at[group, block_rows(block), pl.ds(0, WIDTHS[group])]
                    arrived(piece, ag_s.at[way, s - 1, group], ag_r.at[way, s - 1, group])
                if s < 3 or (s == 3 and way == group):
                    push(*ag_copy(way, s, group))

    def rs_push(way, k, s):
        size = CHUNKS[k][1]
        block = zmod(z + 4 - s) if way == 0 else zmod(z - 4 + s)
        if s == 0:
            piece = back.at[k, block_rows(2 * block + way, 64), pl.ds(0, size)]
            landing = ring.at[way, k, 0, pl.ds(0, 64), pl.ds(0, size)]
        else:
            piece = back.at[k, block_rows(block), pl.ds(0, size)]
            landing = ring.at[way, k, s, :, pl.ds(0, size)]
        push(piece, landing, rs_s.at[way, k, s], rs_r.at[way, k, s], z_next[way])

    def rs_arrived(way, k, s):
        size = CHUNKS[k][1]
        landing = ring.at[way, k, s, pl.ds(0, B if s else 64), pl.ds(0, size)]
        arrived(landing, rs_s.at[way, k, s], rs_r.at[way, k, s])

    def back_step(k, s):
        start, size = CHUNKS[k]
        cols = slice(0, size)
        if s == 0:
            weight_arrived(k)

            def product(m, carry):
                rows = block_rows(m, 256)
                term = dot_t(grads[0, rows, :], w_all[0, start : start + size, :])
                term = term + dot_t(grads[1, rows, :], w_all[1, start : start + size, :])
                back[k, rows, cols] = term.astype(BF16)
                return carry

            lax.fori_loop(0, ROWS // 256, product, 0)
            for way in range(2):
                rs_push(way, k, 0)
        elif s < 4:
            for way in range(2):
                rs_arrived(way, k, s - 1)
                block = zmod(z + 4 - s) if way == 0 else zmod(z - 4 + s)
                if s == 1:
                    rows = block_rows(2 * block + way, 64)
                    came = ring[way, k, 0, :64, cols]
                else:
                    rows = block_rows(block)
                    came = ring[way, k, s - 1, :, cols]
                back[k, rows, cols] = (back[k, rows, cols].astype(F32) + came.astype(F32)).astype(BF16)
                rs_push(way, k, s)
        else:
            for way in range(2):
                rs_arrived(way, k, 3)
            total = back[k, block_rows(z), cols].astype(F32)
            total = total + ring[0, k, 3, :, cols].astype(F32) + ring[1, k, 3, :, cols].astype(F32)
            total = total.astype(BF16)
            for b in range(size // B):
                group, place = divmod(start // B + b, HALF // B)
                rot_grad[group, :, place * B : (place + 1) * B] = total[:, b * B : (b + 1) * B]

    def out_product(turn):
        width = xl if turn == 0 else 1 - xl

        def one(n, carry):
            r = lax.rem(n + 1, 4)
            rows = block_rows(lax.rem(y + r, 4), 256)
            for h in range(2):
                cols = slice(h * 512, (h + 1) * 512)
                term = dot(acts[0, rows, :], w_all[width, :HALF, cols])
                term = term + dot(acts[1, rows, : WIDTHS[1]], w_all[width, HALF:, cols])
                cpart[turn, h, rows, :] = term.astype(BF16)
            copy(cpart.at[turn, 1 - core, rows, :], crecv.at[turn, rows, :], c_s.at[turn, r], c_r.at[turn, r], sibling).start()
            return carry

        lax.fori_loop(0, 4, one, 0)
        for r in range(4):
            rows = block_rows(lax.rem(y + r, 4), 256)
            sent.append(copy(cpart.at[turn, 1 - core, rows, :], crecv.at[turn, rows, :], c_s.at[turn, r], c_r.at[turn, r], sibling))

    def out_core_sum(turn):
        for r in (1, 2, 3, 0):
            rows = block_rows(lax.rem(y + r, 4), 256)
            arrived(crecv.at[turn, rows, :], c_s.at[turn, r], c_r.at[turn, r])
            csum[turn, rows, :] = (cpart[turn, core, rows, :].astype(F32) + crecv[turn, rows, :].astype(F32)).astype(BF16)
            if r:
                push(csum.at[turn, rows, :], yrecv.at[turn, r - 1], y_s.at[turn, r], y_r.at[turn, r], y_peer[r])

    def out_y_part(turn, side):
        total = csum[turn, block_rows(2 * y + side), :].astype(F32)
        for r in range(3):
            total = total + yrecv[turn, r, block_rows(side), :].astype(F32)
        return total

    def out_y_sum(turn):
        for r in range(1, 4):
            arrived(yrecv.at[turn, r - 1], y_s.at[turn, r], y_r.at[turn, r])
        xsend[turn] = out_y_part(turn, 1 - xh).astype(BF16)
        push(xsend.at[turn], xrecv.at[turn], x_s.at[turn], x_r.at[turn], across)

    out_copies = [
        copy(osend.at[0], oacc.at[core], o_s.at[0], o_r.at[core], sibling),
        copy(osend.at[1], oacc.at[core], o_s.at[1], o_r.at[core], dev(xl_=1 - xl, c_=xl)),
    ]

    def out_place(turn):
        arrived(xrecv.at[turn], x_s.at[turn], x_r.at[turn])
        osend[turn] = (out_y_part(turn, xh) + xrecv[turn].astype(F32)).astype(BF16)
        if turn == 0:

            @pl.when(core == xl)
            def _():
                oacc[core] = osend[0]

            @pl.when(core != xl)
            def _():
                out_copies[0].start()
        else:
            out_copies[1].start()

    def out_done():
        @pl.when(core == xl)
        def _():
            arrived(oacc.at[1 - core], o_s.at[0], o_r.at[1 - core])

        @pl.when(core != xl)
        def _():
            for h in range(2):
                arrived(oacc.at[h], o_s.at[0], o_r.at[h])

        for h in range(2):
            out_ref[:, h * 512 : (h + 1) * 512] = oacc[h]

    grad_own()
    scattered(0)
    mix(0)
    gather(0, acts, z * 8)
    grad_across()
    gathered(0, acts, z * 8)
    ag_step(0)
    for r in (1, 3, 2):
        grad_y(0, r)
    ag_step(1)
    for r in (1, 3, 2):
        grad_y(1, r)
    grad_done()
    ag_step(2)
    back_step(0, 0)
    ag_step(3)
    back_step(0, 1)
    back_step(1, 0)
    ag_step(4)
    early = [lambda: out_product(0), lambda: out_core_sum(0), lambda: out_y_sum(0), lambda: out_place(0)]
    n = len(CHUNKS)
    for tick in range(2, n + 4):
        for s in (4, 3, 2, 1, 0):
            k = tick - s
            if 0 <= k < n and (k, s) != (0, 1):
                back_step(k, s)
        if tick == n - 1:
            out_product(1)
        elif tick == n:
            out_core_sum(1)
        elif tick == n + 2:
            out_y_sum(1)
        if early:
            early.pop(0)()
    scatter(1, rot_grad)
    out_place(1)
    scattered(1)
    mix(1)
    gather(1, grad_hid, 0)
    out_done()
    gathered(1, grad_hid, 0)

    def grad_rows(i, carry):
        rows = block_rows(i, 16)
        gate, up = gate_ref[rows, :].astype(F32), up_ref[rows, :].astype(F32)
        sig = jax.nn.sigmoid(gate)
        silu, slope = gate * sig, up * sig * (1.0 + gate * (1.0 - sig))
        for group in range(2):
            cols = slice(group * HALF, group * HALF + WIDTHS[group])
            value = grad_hid[group, rows, : WIDTHS[group]].astype(F32)
            up_grad_ref[rows, cols] = (value * silu[:, cols]).astype(BF16)
            gate_grad_ref[rows, cols] = (value * slope[:, cols]).astype(BF16)
        return carry

    lax.fori_loop(0, 8, grad_rows, 0)

    for op in sent:
        op.wait_send()

    @pl.when(core != xl)
    def _():
        diagonal_copy.wait_send()
        out_copies[0].wait_send()

    out_copies[1].wait_send()

    def drain(j, carry):
        out_copy(0, hid, j).wait_send()
        out_copy(1, rot_grad, j).wait_send()
        back_copy(0, acts, z * 8, j).wait_send()
        back_copy(1, grad_hid, 0, j).wait_send()
        return carry

    lax.fori_loop(1, NT, drain, 0)


def hadamard():
    index = np.arange(B)
    bits = index[:, None] & index[None, :]
    parity = sum(bits >> s & 1 for s in range(7)) % 2
    return (1 - 2 * parity).astype(np.float32)


def on_device(gate_act, up_act, down_codes, down_scales, grad_out):
    vmem, dma = pltpu.VMEM, pltpu.SemaphoreType.DMA
    whole = pl.BlockSpec(memory_space=pltpu.VMEM)
    return pl.pallas_call(
        kernel,
        out_shape=(
            jax.ShapeDtypeStruct((B, DL), BF16),
            jax.ShapeDtypeStruct((B, FL), BF16),
            jax.ShapeDtypeStruct((B, FL), BF16),
        ),
        in_specs=[
            whole,
            whole,
            pl.BlockSpec(memory_space=pl.ANY),
            pl.BlockSpec(memory_space=pltpu.SMEM),
            whole,
            whole,
        ],
        out_specs=(whole, whole, whole),
        scratch_shapes=[
            vmem((FL, DL), BF16),
            vmem((2, FL, DL), BF16),
            vmem((2, B, HALF), BF16),
            vmem((2, NT, 16, HALF), BF16),
            vmem((2, NT, 16, HALF), BF16),
            vmem((2, ROWS, HALF), BF16),
            vmem((2, ROWS, DL), BF16),
            vmem((2, 2, ROWS, 512), BF16),
            vmem((2, ROWS, 512), BF16),
            vmem((2, ROWS, 512), BF16),
            vmem((2, 3, 256, 512), BF16),
            vmem((2, B, 512), BF16),
            vmem((2, B, 512), BF16),
            vmem((2, B, 512), BF16),
            vmem((2, B, 512), BF16),
            vmem((7, ROWS, 256), BF16),
            vmem((2, 7, 4, B, 256), BF16),
            vmem((2, B, HALF), BF16),
            vmem((2, B, HALF), BF16),
            dma,
            dma((7,)), dma((7,)),
            dma((4, NT)), dma((4, NT)),
            dma((2, 4, 2)), dma((2, 4, 2)),
            dma, dma,
            dma, dma,
            dma((2, 4)), dma((2, 4)),
            dma((2, 4)), dma((2, 4)),
            dma((2, 4)), dma((2, 4)),
            dma((2, 4)), dma((2, 4)),
            dma((2,)), dma((2,)),
            dma((2,)), dma((2,)),
            dma((2, 7, 4)), dma((2, 7, 4)),
        ],
        compiler_params=pltpu.CompilerParams(
            collective_id=0, has_side_effects=True, vmem_limit_bytes=56 * 1024 * 1024
        ),
    )(gate_act, up_act, down_codes, down_scales, grad_out, jnp.asarray(hadamard(), BF16))


def solution(mesh):
    return jax.shard_map(
        on_device,
        mesh=mesh,
        in_specs=(
            P("dp", "tensor"),
            P("dp", "tensor"),
            P("tensor", "dp"),
            P("tensor", "dp"),
            P("tensor", "dp"),
        ),
        out_specs=(P("tensor", "dp"), P("dp", "tensor"), P("dp", "tensor")),
        check_vma=False,
    )
```

```python
import math

import jax
import jax.numpy as jnp
import numpy as np
from jax import lax
from jax.experimental import pallas as pl
from jax.experimental.pallas import tpu as pltpu
from jax.sharding import PartitionSpec as P

MESH = pl.DeviceIdType.MESH
F32, BF16 = jnp.float32, jnp.bfloat16
B = 128
FL, DL = 1664, 1024
NZ, NT = 8, 16
HALF = 896
WIDTHS = (896, 768)
ROWS = NZ * B
CHUNKS = ((0, B),) + tuple((B + k * 256, 256) for k in range(6))


def dot(a, b):
    return jnp.dot(a, b, preferred_element_type=F32)


def dot_t(a, b):
    return lax.dot_general(a, b, (((1,), (1,)), ((), ())), preferred_element_type=F32)


def block_rows(index, size=B):
    return pl.ds(pl.multiple_of(index * size, size), size)


def kernel(
    gate_ref, up_ref, codes_ref, scales_ref, grad_ref, had_ref,
    out_ref, grad_ref_out,
    codes_v, w_all, hid, mix_in, mix_out, acts, grads,
    cpart, crecv, csum, yrecv, xsend, xrecv, osend, oacc,
    back, ring, rot_grad, grad_hid,
    code_sem, w_s, w_r, a_s, a_r, ag_s, ag_r,
    gd_s, gd_r, gx_s, gx_r, gy_s, gy_r, gc_s, gc_r,
    c_s, c_r, y_s, y_r, x_s, x_r, o_s, o_r, rs_s, rs_r,
):
    d, t = lax.axis_index("dp"), lax.axis_index("tensor")
    z, xl = lax.div(d, 2), lax.rem(d, 2)
    y, xh, core = lax.div(t, 4), lax.rem(lax.div(t, 2), 2), lax.rem(t, 2)

    def dev(z_=z, xl_=xl, y_=y, xh_=xh, c_=core):
        return (z_ * 2 + xl_, y_ * 4 + xh_ * 2 + c_)

    def zmod(v):
        return lax.rem(v + NZ, NZ)

    partner = dev(xl_=1 - xl)
    diagonal = dev(xl_=1 - xl, c_=1 - core)
    sibling = dev(c_=1 - core)
    across = dev(xh_=1 - xh)
    z_next = (dev(z_=zmod(z + 1)), dev(z_=zmod(z - 1)))
    y_peer = [dev(y_=lax.rem(y + r, 4)) for r in range(4)]
    sent = []

    def copy(src, dst, send, recv, device):
        return pltpu.make_async_remote_copy(
            src_ref=src, dst_ref=dst, send_sem=send, recv_sem=recv, device_id=device, device_id_type=MESH
        )

    def push(*args):
        op = copy(*args)
        op.start()
        sent.append(op)

    def arrived(dst, send, recv):
        copy(dst, dst, send, recv, sibling).wait_recv()

    fetch = pltpu.make_async_copy(codes_ref, codes_v, code_sem)
    fetch.start()

    barrier = pltpu.get_barrier_semaphore()

    def greet(j, carry):
        pl.semaphore_signal(barrier, inc=1, device_id=(d, lax.rem(t + j, NT)), device_id_type=MESH)
        return carry

    lax.fori_loop(1, NT, greet, 0)
    for device in (*z_next, partner, diagonal):
        pl.semaphore_signal(barrier, inc=1, device_id=device, device_id_type=MESH)

    def hidden_rows(i, carry):
        rows = block_rows(i, 16)
        gate = gate_ref[rows, :].astype(F32)
        value = (gate * jax.nn.sigmoid(gate) * up_ref[rows, :].astype(F32)).astype(BF16)
        hid[0, rows, :] = value[:, :HALF]
        hid[1, rows, : WIDTHS[1]] = value[:, HALF:]
        hid[1, rows, WIDTHS[1] :] = jnp.zeros((16, HALF - WIDTHS[1]), BF16)
        rot_grad[1, rows, WIDTHS[1] :] = jnp.zeros((16, HALF - WIDTHS[1]), BF16)
        return carry

    lax.fori_loop(0, 8, hidden_rows, 0)
    pl.semaphore_wait(barrier, NT - 1 + 4)

    def out_copy(i, src, j):
        p = lax.rem(t + j, NT)
        piece = src.at[lax.rem(p, 2), block_rows(lax.div(p, 2), 16), :]
        return copy(piece, mix_in.at[i, t], a_s.at[2 * i, j], a_r.at[2 * i, j], (d, p))

    def scatter(i, src):
        def step(j, carry):
            out_copy(i, src, j).start()
            return carry

        lax.fori_loop(1, NT, step, 0)
        mix_in[i, t] = src[core, block_rows(lax.div(t, 2), 16), :]

    def to_group(group, body):
        other = lax.rem(core + group, 2)

        def step(i, carry):
            body(2 * i + other)
            return carry

        lax.fori_loop(1 - other, NT // 2, step, 0)

    def scatter_group(src, group):
        to_group(group, lambda j: out_copy(1, src, j).start())

        @pl.when(core == group)
        def _():
            mix_in[1, t] = src[core, block_rows(lax.div(t, 2), 16), :]

    def scattered(i):
        def step(j, carry):
            p = lax.rem(t - j + NT, NT)
            arrived(mix_in.at[i, p], a_s.at[2 * i, j], a_r.at[2 * i, j])
            return carry

        lax.fori_loop(1, NT, step, 0)

    def mix(i):
        had = had_ref[...]
        for b in range(HALF // B):
            cols = slice(b * B, (b + 1) * B)
            mixed = dot(mix_in[i, :, :, cols].reshape(256, B), had)
            parts = [mixed[g * 16 : (g + 1) * 16] for g in range(NT)]
            for bit in (1, 2, 4, 8):
                parts = [parts[g] + parts[g ^ bit] if not g & bit else parts[g ^ bit] - parts[g] for g in range(NT)]
            for g in range(NT):
                mix_out[i, g, :, cols] = (parts[g] * (1.0 / math.sqrt(NT * B))).astype(BF16)

    def back_copy(i, dst, base, j):
        p = lax.rem(t + j, NT)
        landing = dst.at[core, block_rows(base + lax.div(t, 2), 16), :]
        return copy(mix_out.at[i, p], landing, a_s.at[2 * i + 1, j], a_r.at[2 * i + 1, j], (d, p))

    def gather(i, dst, base):
        def step(j, carry):
            back_copy(i, dst, base, j).start()
            return carry

        lax.fori_loop(1, NT, step, 0)
        dst[core, block_rows(base + lax.div(t, 2), 16), :] = mix_out[i, t]

    def gathered(i, dst, base):
        def step(j, carry):
            p = lax.rem(t - j + NT, NT)
            landing = dst.at[lax.rem(p, 2), block_rows(base + lax.div(p, 2), 16), :]
            arrived(landing, a_s.at[2 * i + 1, j], a_r.at[2 * i + 1, j])
            return carry

        lax.fori_loop(1, NT, step, 0)

    own_rows, across_rows = block_rows(2 * y + xh), block_rows(2 * y + 1 - xh)
    diagonal_copy = copy(grad_ref, grads.at[xl, own_rows, :], gd_s, gd_r, diagonal)


    def weight_copy(k):
        start, size = CHUNKS[k]
        piece = w_all.at[xl, pl.ds(start, size), :]
        return (piece, piece, w_s.at[k], w_r.at[k], partner)

    def weight_arrived(k):
        start, size = CHUNKS[k]
        arrived(w_all.at[1 - xl, pl.ds(start, size), :], w_s.at[k], w_r.at[k])

    def dequantize(k):
        start, size = CHUNKS[k]

        for i in range(start // B, (start + size) // B):
            rows = slice(i * B, (i + 1) * B)
            for j in range(DL // B):
                cols = slice(j * B, (j + 1) * B)
                scale = jnp.broadcast_to(scales_ref[j : j + 1, i : i + 1], (B, B))
                w_all[xl, rows, cols] = (codes_v[rows, cols].astype(F32) * scale).astype(BF16)

    def grad_own():
        @pl.when(core != xl)
        def _():
            arrived(grads.at[core, own_rows, :], gd_s, gd_r)

        mine = grads.at[core, own_rows, :]
        push(mine, mine, gx_s, gx_r, across)
        for r in (1, 3, 2):
            push(mine, mine, gy_s.at[0, r], gy_r.at[0, r], y_peer[r])
        push(mine, mine, gc_s.at[0, 0], gc_r.at[0, 0], sibling)

    def grad_across():
        piece = grads.at[core, across_rows, :]
        arrived(piece, gx_s, gx_r)
        for r in (1, 3, 2):
            push(piece, piece, gy_s.at[1, r], gy_r.at[1, r], y_peer[r])
        push(piece, piece, gc_s.at[1, 0], gc_r.at[1, 0], sibling)

    def grad_y(f, r):
        source = lax.rem(y - r + 4, 4)
        piece = grads.at[core, block_rows(2 * source + (1 - xh if f else xh)), :]
        arrived(piece, gy_s.at[f, r], gy_r.at[f, r])
        push(piece, piece, gc_s.at[f, r], gc_r.at[f, r], sibling)

    def grad_done():
        for f in range(2):
            for r in range(4):
                source = lax.rem(y - r + 4, 4)
                piece = grads.at[1 - core, block_rows(2 * source + (1 - xh if f else xh)), :]
                arrived(piece, gc_s.at[f, r], gc_r.at[f, r])

    def ag_copy(way, s, group):
        block = zmod(z - s) if way == 0 else zmod(z + s)
        piece = acts.at[group, block_rows(block), pl.ds(0, WIDTHS[group])]
        return (piece, piece, ag_s.at[way, s, group], ag_r.at[way, s, group], z_next[way])

    def ag_step(s):
        for way in range(2):
            for group in range(2):
                if s and (s < 4 or way == group):
                    block = zmod(z - s) if way == 0 else zmod(z + s)
                    piece = acts.at[group, block_rows(block), pl.ds(0, WIDTHS[group])]
                    arrived(piece, ag_s.at[way, s - 1, group], ag_r.at[way, s - 1, group])
                if s < 3 or (s == 3 and way == group):
                    push(*ag_copy(way, s, group))

    def rs_push(way, k, s):
        size = CHUNKS[k][1]
        block = zmod(z + 4 - s) if way == 0 else zmod(z - 4 + s)
        if s == 0:
            piece = back.at[k, block_rows(2 * block + way, 64), pl.ds(0, size)]
            landing = ring.at[way, k, 0, pl.ds(0, 64), pl.ds(0, size)]
        else:
            piece = back.at[k, block_rows(block), pl.ds(0, size)]
            landing = ring.at[way, k, s, :, pl.ds(0, size)]
        push(piece, landing, rs_s.at[way, k, s], rs_r.at[way, k, s], z_next[way])

    def rs_arrived(way, k, s):
        size = CHUNKS[k][1]
        landing = ring.at[way, k, s, pl.ds(0, B if s else 64), pl.ds(0, size)]
        arrived(landing, rs_s.at[way, k, s], rs_r.at[way, k, s])

    def back_step(k, s):
        start, size = CHUNKS[k]
        cols = slice(0, size)
        if s == 0:
            weight_arrived(k)

            def product(m, carry):
                rows = block_rows(m, 256)
                term = dot_t(grads[0, rows, :], w_all[0, start : start + size, :])
                term = term + dot_t(grads[1, rows, :], w_all[1, start : start + size, :])
                back[k, rows, cols] = term.astype(BF16)
                return carry

            lax.fori_loop(0, ROWS // 256, product, 0)
            for way in range(2):
                rs_push(way, k, 0)
        elif s < 4:
            for way in range(2):
                rs_arrived(way, k, s - 1)
                block = zmod(z + 4 - s) if way == 0 else zmod(z - 4 + s)
                if s == 1:
                    rows = block_rows(2 * block + way, 64)
                    came = ring[way, k, 0, :64, cols]
                else:
                    rows = block_rows(block)
                    came = ring[way, k, s - 1, :, cols]
                back[k, rows, cols] = (back[k, rows, cols].astype(F32) + came.astype(F32)).astype(BF16)
                rs_push(way, k, s)
        else:
            for way in range(2):
                rs_arrived(way, k, 3)
            total = back[k, block_rows(z), cols].astype(F32)
            total = total + ring[0, k, 3, :, cols].astype(F32) + ring[1, k, 3, :, cols].astype(F32)
            total = total.astype(BF16)
            for b in range(size // B):
                group, place = divmod(start // B + b, HALF // B)
                rot_grad[group, :, place * B : (place + 1) * B] = total[:, b * B : (b + 1) * B]

    def out_core_copy(turn, r):
        rows = block_rows(lax.rem(y + r, 4), 256)
        return (cpart.at[turn, 1 - core, rows, :], crecv.at[turn, rows, :], c_s.at[turn, r], c_r.at[turn, r], sibling)

    def out_product(turn, r):
        width = xl if turn == 0 else 1 - xl
        rows = block_rows(lax.rem(y + r, 4), 256)
        for h in range(2):
            cols = slice(h * 512, (h + 1) * 512)
            term = dot(acts[0, rows, :], w_all[width, :HALF, cols])
            term = term + dot(acts[1, rows, : WIDTHS[1]], w_all[width, HALF:, cols])
            cpart[turn, h, rows, :] = term.astype(BF16)
        push(*out_core_copy(turn, r))

    def out_core_sum(turn, r):
        rows = block_rows(lax.rem(y + r, 4), 256)
        arrived(crecv.at[turn, rows, :], c_s.at[turn, r], c_r.at[turn, r])
        csum[turn, rows, :] = (cpart[turn, core, rows, :].astype(F32) + crecv[turn, rows, :].astype(F32)).astype(BF16)
        if r:
            push(csum.at[turn, rows, :], yrecv.at[turn, r - 1], y_s.at[turn, r], y_r.at[turn, r], y_peer[r])

    def out_y_part(turn, side):
        total = csum[turn, block_rows(2 * y + side), :].astype(F32)
        for r in range(3):
            total = total + yrecv[turn, r, block_rows(side), :].astype(F32)
        return total

    def out_y_sum(turn):
        for r in range(1, 4):
            arrived(yrecv.at[turn, r - 1], y_s.at[turn, r], y_r.at[turn, r])
        xsend[turn] = out_y_part(turn, 1 - xh).astype(BF16)
        push(xsend.at[turn], xrecv.at[turn], x_s.at[turn], x_r.at[turn], across)

    out_copies = [
        copy(osend.at[0], oacc.at[core], o_s.at[0], o_r.at[core], sibling),
        copy(osend.at[1], oacc.at[core], o_s.at[1], o_r.at[core], dev(xl_=1 - xl, c_=xl)),
    ]

    def out_place(turn):
        arrived(xrecv.at[turn], x_s.at[turn], x_r.at[turn])
        osend[turn] = (out_y_part(turn, xh) + xrecv[turn].astype(F32)).astype(BF16)
        if turn == 0:

            @pl.when(core == xl)
            def _():
                oacc[core] = osend[0]

            @pl.when(core != xl)
            def _():
                out_copies[0].start()
        else:
            out_copies[1].start()

    def out_done():
        @pl.when(core == xl)
        def _():
            arrived(oacc.at[1 - core], o_s.at[0], o_r.at[1 - core])

        @pl.when(core != xl)
        def _():
            for h in range(2):
                arrived(oacc.at[h], o_s.at[0], o_r.at[h])

    scatter(0, hid)

    @pl.when(core != xl)
    def _():
        diagonal_copy.start()

    @pl.when(core == xl)
    def _():
        grads[core, own_rows, :] = grad_ref[...]

    fetch.wait()
    dequantize(0)
    push(*weight_copy(0))
    for k in range(1, 7):
        dequantize(k)
    grad_own()
    scattered(0)
    mix(0)
    gather(0, acts, z * 8)
    for k in range(1, 7):
        push(*weight_copy(k))
    grad_across()
    gathered(0, acts, z * 8)
    ag_step(0)
    for r in (1, 3, 2):
        grad_y(0, r)
    ag_step(1)
    for r in (1, 3, 2):
        grad_y(1, r)
    grad_done()
    ag_step(2)
    back_step(0, 0)
    ag_step(3)
    back_step(0, 1)
    back_step(1, 0)
    ag_step(4)
    n = len(CHUNKS)

    def tick(i):
        for s in (4, 3, 2, 1, 0):
            if 0 <= i - s < n and (i - s, s) != (0, 1):
                back_step(i - s, s)

    tick(2)
    for r in (1, 2):
        out_product(0, r)
    tick(3)
    for r in (3, 0):
        out_product(0, r)
    for r in (1, 2):
        out_core_sum(0, r)
    tick(4)
    for r in (3, 0):
        out_core_sum(0, r)
    tick(5)
    out_y_sum(0)
    tick(6)
    out_product(1, 1)
    tick(7)
    scatter_group(rot_grad, 0)
    out_core_sum(1, 1)
    out_product(1, 2)
    tick(8)
    out_core_sum(1, 2)
    out_product(1, 3)
    tick(9)
    out_core_sum(1, 3)
    out_product(1, 0)

    @pl.when(core == 0)
    def _():
        scattered(1)
        mix(1)
        gather(1, grad_hid, 0)

    tick(10)
    scatter_group(rot_grad, 1)
    out_core_sum(1, 0)
    out_y_sum(1)
    out_place(0)

    @pl.when(core == 1)
    def _():
        scattered(1)
        mix(1)
        gather(1, grad_hid, 0)

    out_place(1)
    out_done()
    gathered(1, grad_hid, 0)
    for h in range(2):
        out_ref[:, h * 512 : (h + 1) * 512] = oacc[h]
    grad_ref_out[:, :HALF] = grad_hid[0]
    grad_ref_out[:, HALF:] = grad_hid[1, :, : WIDTHS[1]]

    for op in sent:
        op.wait_send()

    @pl.when(core != xl)
    def _():
        diagonal_copy.wait_send()
        out_copies[0].wait_send()

    out_copies[1].wait_send()

    def drain(j, carry):
        out_copy(0, hid, j).wait_send()
        out_copy(1, rot_grad, j).wait_send()
        back_copy(0, acts, z * 8, j).wait_send()
        back_copy(1, grad_hid, 0, j).wait_send()
        return carry

    lax.fori_loop(1, NT, drain, 0)


def hadamard():
    index = np.arange(B)
    bits = index[:, None] & index[None, :]
    parity = sum(bits >> s & 1 for s in range(7)) % 2
    return (1 - 2 * parity).astype(np.float32)


def on_device(gate_act, up_act, down_codes, down_scales, grad_out):
    vmem, dma = pltpu.VMEM, pltpu.SemaphoreType.DMA
    whole = pl.BlockSpec(memory_space=pltpu.VMEM)
    layer_output, grad_hidden = pl.pallas_call(
        kernel,
        out_shape=(jax.ShapeDtypeStruct((B, DL), BF16), jax.ShapeDtypeStruct((B, FL), BF16)),
        in_specs=[whole, whole, pl.BlockSpec(memory_space=pl.ANY), whole, whole, whole],
        out_specs=(whole, whole),
        scratch_shapes=[
            vmem((FL, DL), BF16),
            vmem((2, FL, DL), BF16),
            vmem((2, B, HALF), BF16),
            vmem((2, NT, 16, HALF), BF16),
            vmem((2, NT, 16, HALF), BF16),
            vmem((2, ROWS, HALF), BF16),
            vmem((2, ROWS, DL), BF16),
            vmem((2, 2, ROWS, 512), BF16),
            vmem((2, ROWS, 512), BF16),
            vmem((2, ROWS, 512), BF16),
            vmem((2, 3, 256, 512), BF16),
            vmem((2, B, 512), BF16),
            vmem((2, B, 512), BF16),
            vmem((2, B, 512), BF16),
            vmem((2, B, 512), BF16),
            vmem((7, ROWS, 256), BF16),
            vmem((2, 7, 4, B, 256), BF16),
            vmem((2, B, HALF), BF16),
            vmem((2, B, HALF), BF16),
            dma,
            dma((7,)), dma((7,)),
            dma((4, NT)), dma((4, NT)),
            dma((2, 4, 2)), dma((2, 4, 2)),
            dma, dma,
            dma, dma,
            dma((2, 4)), dma((2, 4)),
            dma((2, 4)), dma((2, 4)),
            dma((2, 4)), dma((2, 4)),
            dma((2, 4)), dma((2, 4)),
            dma((2,)), dma((2,)),
            dma((2,)), dma((2,)),
            dma((2, 7, 4)), dma((2, 7, 4)),
        ],
        compiler_params=pltpu.CompilerParams(
            collective_id=0, has_side_effects=True, vmem_limit_bytes=56 * 1024 * 1024
        ),
    )(gate_act, up_act, down_codes, down_scales.T, grad_out, jnp.asarray(hadamard(), BF16))
    grad_hidden = grad_hidden.astype(F32)
    gate, up = gate_act.astype(F32), up_act.astype(F32)
    sig = jax.nn.sigmoid(gate)
    up_grad = (grad_hidden * (gate * sig)).astype(BF16)
    gate_grad = (grad_hidden * up * sig * (1.0 + gate * (1.0 - sig))).astype(BF16)
    return (layer_output, gate_grad, up_grad)


def solution(mesh):
    return jax.shard_map(
        on_device,
        mesh=mesh,
        in_specs=(
            P("dp", "tensor"),
            P("dp", "tensor"),
            P("tensor", "dp"),
            P("tensor", "dp"),
            P("tensor", "dp"),
        ),
        out_specs=(P("tensor", "dp"), P("dp", "tensor"), P("dp", "tensor")),
        check_vma=False,
    )
```

```python
import math

import jax
import jax.numpy as jnp
import numpy as np
from jax import lax
from jax.experimental import pallas as pl
from jax.experimental.pallas import tpu as pltpu
from jax.sharding import PartitionSpec as P

MESH = pl.DeviceIdType.MESH
F32, BF16 = jnp.float32, jnp.bfloat16
B = 128
FL, DL = 1664, 1024
NZ, NT = 8, 16
HALF = 896
WIDTHS = (896, 768)
ROWS = NZ * B
STRIPS = ((0, 256), (256, 256), (512, 256), (768, B), (896, 256), (1152, 256), (1408, B), (1536, B))
ORDER = tuple((k, h) for k in range(6) for h in range(2)) + tuple((k, h) for h in range(2) for k in range(6, 8))
CHUNKS = ((0, 512), (512, 384), (896, 256), (1152, 256), (1408, B), (1536, B))
STRIPS_OF = ((0, 1), (2, 3), (4,), (5,), (6,), (7,))
RING = 4
TURNS = ((0, 0, 512), (1, 0, 256), (1, 512, 256))
PIECES = ((0, 0, 896), (1, 0, 512), (1, 512, 256))


def dot(a, b):
    return jnp.dot(a, b, preferred_element_type=F32)


def dot_t(a, b):
    return lax.dot_general(a, b, (((1,), (1,)), ((), ())), preferred_element_type=F32)


def block_rows(index, size=B):
    return pl.ds(pl.multiple_of(index * size, size), size)


def kernel(
    gate_hbm, up_hbm, codes_hbm, scales_hbm, grad_hbm, had_hbm,
    out_ref, grad_ref_out,
    gate_ref, up_ref, codes_v, scales_ref, grad_ref, had_ref,
    w_all, hid, mix_in, mix_out, acts, grads,
    cpart, crecv, csum, yrecv, xsend, xrecv, osend, oacc,
    back0, back1, back2, back3, ring0, ring1, ring2, ring3, back_last, direct, rot_grad, grad_hid,
    in_sem, w_s, w_r, a_s, a_r, e_s, e_r, ag_s, ag_r,
    gd_s, gd_r, gx_s, gx_r, gy_s, gy_r, gc_s, gc_r,
    c_s, c_r, y_s, y_r, x_s, x_r, o_s, o_r, rs_s, rs_r, ds_s, ds_r,
):
    d, t = lax.axis_index("dp"), lax.axis_index("tensor")
    back, ring = (back0, back1, back2, back3), (ring0, ring1, ring2, ring3)
    z, xl = lax.div(d, 2), lax.rem(d, 2)
    y, xh, core = lax.div(t, 4), lax.rem(lax.div(t, 2), 2), lax.rem(t, 2)

    def dev(z_=z, xl_=xl, y_=y, xh_=xh, c_=core):
        return (z_ * 2 + xl_, y_ * 4 + xh_ * 2 + c_)

    def zmod(v):
        return lax.rem(v + NZ, NZ)

    partner = dev(xl_=1 - xl)
    diagonal = dev(xl_=1 - xl, c_=1 - core)
    sibling = dev(c_=1 - core)
    across = dev(xh_=1 - xh)
    z_next = (dev(z_=zmod(z + 1)), dev(z_=zmod(z - 1)))
    y_peer = [dev(y_=lax.rem(y + r, 4)) for r in range(4)]
    sent = []

    def copy(src, dst, send, recv, device):
        return pltpu.make_async_remote_copy(
            src_ref=src, dst_ref=dst, send_sem=send, recv_sem=recv, device_id=device, device_id_type=MESH
        )

    def push(*args):
        op = copy(*args)
        op.start()
        sent.append(op)

    def arrived(dst, send, recv):
        copy(dst, dst, send, recv, sibling).wait_recv()

    first = pl.ds(0, STRIPS[0][1])
    rest = pl.ds(STRIPS[0][1], FL - STRIPS[0][1])
    fetches = [
        pltpu.make_async_copy(src, dst, in_sem.at[i])
        for i, (src, dst) in enumerate((
            (scales_hbm, scales_ref),
            (codes_hbm.at[first, :], codes_v.at[first, :]),
            (gate_hbm, gate_ref),
            (up_hbm, up_ref),
            (grad_hbm, grad_ref),
            (codes_hbm.at[rest, :], codes_v.at[rest, :]),
            (had_hbm, had_ref),
        ))
    ]
    for fetch in fetches:
        fetch.start()

    barrier = pltpu.get_barrier_semaphore()

    def greet(j, carry):
        pl.semaphore_signal(barrier, inc=1, device_id=(d, lax.rem(t + j, NT)), device_id_type=MESH)
        return carry

    lax.fori_loop(1, NT, greet, 0)
    z_peer = [dev(z_=lax.rem(z + j, NZ)) for j in range(NZ)]
    for device in (*z_peer[1:], partner, diagonal):
        pl.semaphore_signal(barrier, inc=1, device_id=device, device_id_type=MESH)

    def weight_piece(width, k, h):
        start, size = STRIPS[k]
        return w_all.at[width, pl.ds(start, size), pl.ds(h * 512, 512)]

    def weight_push(k, h):
        push(weight_piece(xl, k, h), weight_piece(xl, k, h), w_s.at[h, k], w_r.at[h, k], partner)

    def weight_arrived(k, h):
        arrived(weight_piece(1 - xl, k, h), w_s.at[h, k], w_r.at[h, k])

    def dequantize(k):
        start, size = STRIPS[k]
        for i in range(start // B, (start + size) // B):
            rows = slice(i * B, (i + 1) * B)
            for j in range(DL // B):
                cols = slice(j * B, (j + 1) * B)
                scale = jnp.broadcast_to(scales_ref[j : j + 1, i : i + 1], (B, B))
                w_all[xl, rows, cols] = (codes_v[rows, cols].astype(F32) * scale).astype(BF16)

    fetches[0].wait()
    fetches[1].wait()
    dequantize(0)
    fetches[2].wait()
    fetches[3].wait()

    def hidden_rows(i, carry):
        rows = block_rows(i, 16)
        gate = gate_ref[rows, :].astype(F32)
        value = (gate * jax.nn.sigmoid(gate) * up_ref[rows, :].astype(F32)).astype(BF16)
        hid[0, rows, :] = value[:, :HALF]
        hid[1, rows, : WIDTHS[1]] = value[:, HALF:]
        hid[1, rows, WIDTHS[1] :] = jnp.zeros((16, HALF - WIDTHS[1]), BF16)
        rot_grad[1, rows, WIDTHS[1] :] = jnp.zeros((16, HALF - WIDTHS[1]), BF16)
        return carry

    lax.fori_loop(0, 8, hidden_rows, 0)
    pl.semaphore_wait(barrier, NT - 1 + NZ - 1 + 2)

    def sixteen(p):
        return block_rows(lax.div(p, 2), 16)

    def peers(body):
        def step(j, carry):
            body(j)
            return carry

        lax.fori_loop(1, NT, step, 0)

    def peers_of(group, body):
        other = lax.rem(core + group, 2)

        def step(i, carry):
            body(2 * i + other)
            return carry

        lax.fori_loop(1 - other, NT // 2, step, 0)

    def mix(i, start, size):
        had = had_ref[...]
        for b in range(start // B, (start + size) // B):
            cols = slice(b * B, (b + 1) * B)
            mixed = dot(mix_in[i, :, :, cols].reshape(256, B), had)
            parts = [mixed[g * 16 : (g + 1) * 16] for g in range(NT)]
            for bit in (1, 2, 4, 8):
                parts = [parts[g] + parts[g ^ bit] if not g & bit else parts[g ^ bit] - parts[g] for g in range(NT)]
            for g in range(NT):
                mix_out[i, g, :, cols] = (parts[g] * (1.0 / math.sqrt(NT * B))).astype(BF16)

    def first_copy(j):
        p = lax.rem(t + j, NT)
        return copy(hid.at[lax.rem(p, 2), sixteen(p), :], mix_in.at[0, t], a_s.at[0, j], a_r.at[0, j], (d, p))

    def first_back(j):
        p = lax.rem(t + j, NT)
        landing = acts.at[core, block_rows(z * 8 + lax.div(t, 2), 16), :]
        return copy(mix_out.at[0, p], landing, a_s.at[1, j], a_r.at[1, j], (d, p))

    def first_scatter():
        peers(lambda j: first_copy(j).start())
        mix_in[0, t] = hid[core, sixteen(t), :]

    def first_mix():
        def came(j):
            arrived(mix_in.at[0, lax.rem(t - j + NT, NT)], a_s.at[0, j], a_r.at[0, j])

        peers(came)
        mix(0, 0, HALF)
        peers(lambda j: first_back(j).start())
        acts[core, block_rows(z * 8 + lax.div(t, 2), 16), :] = mix_out[0, t]

    def first_done():
        def came(j):
            p = lax.rem(t - j + NT, NT)
            landing = acts.at[lax.rem(p, 2), block_rows(z * 8 + lax.div(p, 2), 16), :]
            arrived(landing, a_s.at[1, j], a_r.at[1, j])

        peers(came)

    def last_copy(piece, j):
        group, start, size = PIECES[piece]
        p, cols = lax.rem(t + j, NT), pl.ds(start, size)
        src = rot_grad.at[group, sixteen(p), cols]
        return copy(src, mix_in.at[1, t, :, cols], e_s.at[0, piece, j], e_r.at[0, piece, j], (d, p))

    def last_back(piece, j):
        group, start, size = PIECES[piece]
        p, cols = lax.rem(t + j, NT), pl.ds(start, size)
        landing = grad_hid.at[group, sixteen(t), cols]
        return copy(mix_out.at[1, p, :, cols], landing, e_s.at[1, piece, j], e_r.at[1, piece, j], (d, p))

    def last_scatter(piece):
        group, start, size = PIECES[piece]
        peers_of(group, lambda j: last_copy(piece, j).start())

        @pl.when(core == group)
        def _():
            mix_in[1, t, :, start : start + size] = rot_grad[group, sixteen(t), start : start + size]

    def last_mix(piece):
        group, start, size = PIECES[piece]

        def came(j):
            landing = mix_in.at[1, lax.rem(t - j + NT, NT), :, pl.ds(start, size)]
            arrived(landing, e_s.at[0, piece, j], e_r.at[0, piece, j])

        @pl.when(core == group)
        def _():
            peers(came)
            mix(1, start, size)
            peers(lambda j: last_back(piece, j).start())
            grad_hid[group, sixteen(t), start : start + size] = mix_out[1, t, :, start : start + size]

    def last_done():
        for piece, (group, start, size) in enumerate(PIECES):

            def came(j):
                p = lax.rem(t - j + NT, NT)
                landing = grad_hid.at[group, sixteen(p), pl.ds(start, size)]
                arrived(landing, e_s.at[1, piece, j], e_r.at[1, piece, j])

            peers_of(group, came)

    def drain():
        peers(lambda j: first_copy(j).wait_send())
        peers(lambda j: first_back(j).wait_send())
        for piece, (group, _, _) in enumerate(PIECES):
            peers_of(group, lambda j: last_copy(piece, j).wait_send())

            @pl.when(core == group)
            def _():
                peers(lambda j: last_back(piece, j).wait_send())

    own_rows, across_rows = block_rows(2 * y + xh), block_rows(2 * y + 1 - xh)
    diagonal_copy = copy(grad_ref, grads.at[xl, own_rows, :], gd_s, gd_r, diagonal)

    def grad_own():
        @pl.when(core != xl)
        def _():
            arrived(grads.at[core, own_rows, :], gd_s, gd_r)

        mine = grads.at[core, own_rows, :]
        push(mine, mine, gx_s, gx_r, across)
        for r in (1, 3, 2):
            push(mine, mine, gy_s.at[0, r], gy_r.at[0, r], y_peer[r])
        push(mine, mine, gc_s.at[0, 0], gc_r.at[0, 0], sibling)

    def grad_across():
        piece = grads.at[core, across_rows, :]
        arrived(piece, gx_s, gx_r)
        for r in (1, 3, 2):
            push(piece, piece, gy_s.at[1, r], gy_r.at[1, r], y_peer[r])
        push(piece, piece, gc_s.at[1, 0], gc_r.at[1, 0], sibling)

    def grad_y(f, r):
        source = lax.rem(y - r + 4, 4)
        piece = grads.at[core, block_rows(2 * source + (1 - xh if f else xh)), :]
        arrived(piece, gy_s.at[f, r], gy_r.at[f, r])
        push(piece, piece, gc_s.at[f, r], gc_r.at[f, r], sibling)

    def grad_done():
        for f in range(2):
            for r in range(4):
                source = lax.rem(y - r + 4, 4)
                piece = grads.at[1 - core, block_rows(2 * source + (1 - xh if f else xh)), :]
                arrived(piece, gc_s.at[f, r], gc_r.at[f, r])

    def ag_copy(way, s, group):
        block = zmod(z - s) if way == 0 else zmod(z + s)
        piece = acts.at[group, block_rows(block), pl.ds(0, WIDTHS[group])]
        return (piece, piece, ag_s.at[way, s, group], ag_r.at[way, s, group], z_next[way])

    def ag_step(s):
        for way in range(2):
            for group in range(2):
                if s and (s < 4 or way == group):
                    block = zmod(z - s) if way == 0 else zmod(z + s)
                    piece = acts.at[group, block_rows(block), pl.ds(0, WIDTHS[group])]
                    arrived(piece, ag_s.at[way, s - 1, group], ag_r.at[way, s - 1, group])
                if s < 3 or (s == 3 and way == group):
                    push(*ag_copy(way, s, group))

    def rs_push(way, k, s):
        block = zmod(z + 4 - s) if way == 0 else zmod(z - 4 + s)
        if s == 0:
            piece = back[k].at[block_rows(2 * block + way, 64), :]
            landing = ring[k].at[way, 0, pl.ds(0, 64), :]
        else:
            piece = back[k].at[block_rows(block), :]
            landing = ring[k].at[way, s]
        push(piece, landing, rs_s.at[way, k, s], rs_r.at[way, k, s], z_next[way])

    def rs_arrived(way, k, s):
        landing = ring[k].at[way, s, pl.ds(0, B if s else 64), :]
        arrived(landing, rs_s.at[way, k, s], rs_r.at[way, k, s])

    def product(k, h):
        start, size = CHUNKS[k]
        units = slice(start, start + size)
        for strip in STRIPS_OF[k]:
            for part in (0, 1) if h is None else (h,):
                weight_arrived(strip, part)

        def one(m, carry):
            rows = block_rows(m, 256)
            if h == 1:
                term = back[k][rows, :] if k < RING else back_last[k - RING, rows, :]
                term = term.astype(F32) + dot_t(grads[1 - xl, rows, 512:], w_all[1 - xl, units, 512:])
            else:
                seen = slice(0, 512 if h == 0 else DL)
                term = dot_t(grads[xl, rows, :], w_all[xl, units, :])
                term = term + dot_t(grads[1 - xl, rows, seen], w_all[1 - xl, units, seen])
            if k < RING:
                back[k][rows, :] = term.astype(BF16)
            else:
                back_last[k - RING, rows, :] = term.astype(BF16)
            return carry

        lax.fori_loop(0, ROWS // 256, one, 0)

    def back_total(k, arrivals):
        start, size = CHUNKS[k]
        mine = back[k][block_rows(z), :] if k < RING else back_last[k - RING, block_rows(z), :]
        total = mine.astype(F32)
        for came in arrivals:
            total = total + came.astype(F32)
        total = total.astype(BF16)
        for b in range(size // B):
            group, place = divmod(start // B + b, HALF // B)
            rot_grad[group, :, place * B : (place + 1) * B] = total[:, b * B : (b + 1) * B]

    def back_step(k, s):
        if s == 0:
            product(k, None)
            for way in range(2):
                rs_push(way, k, 0)
        elif s < 4:
            for way in range(2):
                rs_arrived(way, k, s - 1)
                block = zmod(z + 4 - s) if way == 0 else zmod(z - 4 + s)
                if s == 1:
                    rows = block_rows(2 * block + way, 64)
                    came = ring[k][way, 0, :64, :]
                else:
                    rows = block_rows(block)
                    came = ring[k][way, s - 1]
                back[k][rows, :] = (back[k][rows, :].astype(F32) + came.astype(F32)).astype(BF16)
                rs_push(way, k, s)
        else:
            for way in range(2):
                rs_arrived(way, k, 3)
            back_total(k, [ring[k][way, 3] for way in range(2)])

    def direct_step(k, s):
        i = k - RING
        if s == 0:
            product(k, 1)
            for j in (4, 3, 5, 2, 6, 1, 7):
                piece = back_last.at[i, block_rows(zmod(z + j)), :]
                push(piece, direct.at[i, j - 1], ds_s.at[i, j], ds_r.at[i, j], z_peer[j])
        else:
            for j in range(1, NZ):
                arrived(direct.at[i, j - 1], ds_s.at[i, j], ds_r.at[i, j])
            back_total(k, [direct[i, j - 1] for j in range(1, NZ)])

    def out_rows(r):
        return block_rows(lax.rem(y + r, 4), 256)

    def out_product(turn, r):
        late, start, size = TURNS[turn]
        width = 1 - xl if late else xl
        rows, share = out_rows(r), pl.ds(0, size)
        for h in range(2):
            cols = slice(start + h * size, start + (h + 1) * size)
            term = dot(acts[0, rows, :], w_all[width, :HALF, cols])
            term = term + dot(acts[1, rows, : WIDTHS[1]], w_all[width, HALF:, cols])
            cpart[turn, h, rows, :size] = term.astype(BF16)
        landing = crecv.at[turn, rows, share]
        push(cpart.at[turn, 1 - core, rows, share], landing, c_s.at[turn, r], c_r.at[turn, r], sibling)

    def out_core_sum(turn, r):
        size = TURNS[turn][2]
        rows, share = out_rows(r), pl.ds(0, size)
        arrived(crecv.at[turn, rows, share], c_s.at[turn, r], c_r.at[turn, r])
        total = cpart[turn, core, rows, :size].astype(F32) + crecv[turn, rows, :size].astype(F32)
        csum[turn, rows, :size] = total.astype(BF16)
        if r:
            landing = yrecv.at[turn, r - 1, :, share]
            push(csum.at[turn, rows, share], landing, y_s.at[turn, r], y_r.at[turn, r], y_peer[r])

    def out_y_part(turn, side):
        size = TURNS[turn][2]
        total = csum[turn, block_rows(2 * y + side), :size].astype(F32)
        for r in range(3):
            total = total + yrecv[turn, r, block_rows(side), :size].astype(F32)
        return total

    def out_y_sum(turn):
        size = TURNS[turn][2]
        share = pl.ds(0, size)
        for r in range(1, 4):
            arrived(yrecv.at[turn, r - 1, :, share], y_s.at[turn, r], y_r.at[turn, r])
        xsend[turn, :, :size] = out_y_part(turn, 1 - xh).astype(BF16)
        push(xsend.at[turn, :, share], xrecv.at[turn, :, share], x_s.at[turn], x_r.at[turn], across)

    def out_cols(turn, sender):
        _, start, size = TURNS[turn]
        return pl.ds(pl.multiple_of(start + sender * size, 256), size)

    def out_copy(turn):
        device = dev(xl_=1 - xl, c_=xl) if turn else sibling
        share = pl.ds(0, TURNS[turn][2])
        return copy(osend.at[turn, :, share], oacc.at[:, out_cols(turn, core)], o_s.at[turn], o_r.at[turn, core], device)

    def out_place(turn):
        size = TURNS[turn][2]
        arrived(xrecv.at[turn, :, pl.ds(0, size)], x_s.at[turn], x_r.at[turn])
        osend[turn, :, :size] = (out_y_part(turn, xh) + xrecv[turn, :, :size].astype(F32)).astype(BF16)
        if turn == 0:

            @pl.when(core == xl)
            def _():
                oacc[:, out_cols(0, core)] = osend[0]

            @pl.when(core != xl)
            def _():
                out_copy(0).start()
        else:
            out_copy(turn).start()

    def out_done():
        @pl.when(core == xl)
        def _():
            arrived(oacc.at[:, out_cols(0, 1 - core)], o_s.at[0], o_r.at[0, 1 - core])

        @pl.when(core != xl)
        def _():
            for turn in (1, 2):
                for sender in range(2):
                    arrived(oacc.at[:, out_cols(turn, sender)], o_s.at[turn], o_r.at[turn, sender])

    first_scatter()
    weight_push(0, 0)
    fetches[4].wait()

    @pl.when(core != xl)
    def _():
        diagonal_copy.start()

    @pl.when(core == xl)
    def _():
        grads[core, own_rows, :] = grad_ref[...]

    fetches[5].wait()
    for k in range(1, len(STRIPS)):
        dequantize(k)
    fetches[6].wait()
    first_mix()
    grad_own()
    for k, h in ORDER[1:]:
        weight_push(k, h)
    first_done()
    ag_step(0)
    grad_across()
    for r in (1, 3, 2):
        grad_y(0, r)
    ag_step(1)
    for r in (1, 3, 2):
        grad_y(1, r)
    grad_done()

    starts = (0, 2, 4, 6)

    def tick(i):
        for s in (4, 3, 2, 1, 0):
            if i - s in starts:
                back_step(starts.index(i - s), s)

    tick(0)
    ag_step(2)
    tick(1)
    ag_step(3)
    tick(2)
    ag_step(4)
    tick(3)
    out_product(0, 1)
    out_product(0, 2)
    tick(4)
    out_product(0, 3)
    out_product(0, 0)
    out_core_sum(0, 1)
    out_core_sum(0, 2)
    tick(5)
    out_core_sum(0, 3)
    out_core_sum(0, 0)
    tick(6)
    last_scatter(0)
    for k in (4, 5):
        product(k, 0)
    tick(7)
    for r in (1, 2, 3, 0):
        out_product(1, r)
    direct_step(4, 0)
    tick(8)
    for r in (1, 2, 3, 0):
        out_core_sum(1, r)
    direct_step(5, 0)
    out_y_sum(0)
    for r in (1, 2, 3, 0):
        out_product(2, r)
    tick(9)
    for r in (1, 2, 3, 0):
        out_core_sum(2, r)
    last_mix(0)
    tick(10)
    last_scatter(1)
    out_y_sum(1)
    out_place(0)
    direct_step(4, 1)
    direct_step(5, 1)
    last_scatter(2)
    out_place(1)
    out_y_sum(2)
    last_mix(1)
    last_mix(2)
    out_place(2)
    out_done()
    last_done()
    out_ref[...] = oacc[...]
    grad_ref_out[:, :HALF] = grad_hid[0]
    grad_ref_out[:, HALF:] = grad_hid[1, :, : WIDTHS[1]]

    for op in sent:
        op.wait_send()

    @pl.when(core != xl)
    def _():
        diagonal_copy.wait_send()
        out_copy(0).wait_send()

    out_copy(1).wait_send()
    out_copy(2).wait_send()
    drain()


def hadamard():
    index = np.arange(B)
    bits = index[:, None] & index[None, :]
    parity = sum(bits >> s & 1 for s in range(7)) % 2
    return (1 - 2 * parity).astype(np.float32)


def on_device(gate_act, up_act, down_codes, down_scales, grad_out):
    vmem, dma = pltpu.VMEM, pltpu.SemaphoreType.DMA
    whole = pl.BlockSpec(memory_space=pltpu.VMEM)
    layer_output, grad_hidden = pl.pallas_call(
        kernel,
        out_shape=(jax.ShapeDtypeStruct((B, DL), BF16), jax.ShapeDtypeStruct((B, FL), BF16)),
        in_specs=[pl.BlockSpec(memory_space=pl.ANY)] * 6,
        out_specs=(whole, whole),
        scratch_shapes=[
            vmem((B, FL), BF16),
            vmem((B, FL), BF16),
            vmem((FL, DL), BF16),
            vmem((DL // B, FL // B), F32),
            vmem((B, DL), BF16),
            vmem((B, B), BF16),
            vmem((2, FL, DL), BF16),
            vmem((2, B, HALF), BF16),
            vmem((2, NT, 16, HALF), BF16),
            vmem((2, NT, 16, HALF), BF16),
            vmem((2, ROWS, HALF), BF16),
            vmem((2, ROWS, DL), BF16),
            vmem((3, 2, ROWS, 512), BF16),
            vmem((3, ROWS, 512), BF16),
            vmem((3, ROWS, 512), BF16),
            vmem((3, 3, 256, 512), BF16),
            vmem((3, B, 512), BF16),
            vmem((3, B, 512), BF16),
            vmem((3, B, 512), BF16),
            vmem((B, DL), BF16),
            *(vmem((ROWS, size), BF16) for _, size in CHUNKS[:RING]),
            *(vmem((2, 4, B, size), BF16) for _, size in CHUNKS[:RING]),
            vmem((len(CHUNKS) - RING, ROWS, B), BF16),
            vmem((len(CHUNKS) - RING, NZ - 1, B, B), BF16),
            vmem((2, B, HALF), BF16),
            vmem((2, B, HALF), BF16),
            dma((7,)),
            dma((2, len(STRIPS))), dma((2, len(STRIPS))),
            dma((2, NT)), dma((2, NT)),
            dma((2, 3, NT)), dma((2, 3, NT)),
            dma((2, 4, 2)), dma((2, 4, 2)),
            dma, dma,
            dma, dma,
            dma((2, 4)), dma((2, 4)),
            dma((2, 4)), dma((2, 4)),
            dma((3, 4)), dma((3, 4)),
            dma((3, 4)), dma((3, 4)),
            dma((3,)), dma((3,)),
            dma((3,)), dma((3, 2)),
            dma((2, RING, 4)), dma((2, RING, 4)),
            dma((2, NZ)), dma((2, NZ)),
        ],
        compiler_params=pltpu.CompilerParams(
            collective_id=0, has_side_effects=True, vmem_limit_bytes=56 * 1024 * 1024
        ),
    )(gate_act, up_act, down_codes, down_scales.T, grad_out, jnp.asarray(hadamard(), BF16))
    grad_hidden = grad_hidden.astype(F32)
    gate, up = gate_act.astype(F32), up_act.astype(F32)
    sig = jax.nn.sigmoid(gate)
    up_grad = (grad_hidden * (gate * sig)).astype(BF16)
    gate_grad = (grad_hidden * up * sig * (1.0 + gate * (1.0 - sig))).astype(BF16)
    return (layer_output, gate_grad, up_grad)


def solution(mesh):
    return jax.shard_map(
        on_device,
        mesh=mesh,
        in_specs=(
            P("dp", "tensor"),
            P("dp", "tensor"),
            P("tensor", "dp"),
            P("tensor", "dp"),
            P("tensor", "dp"),
        ),
        out_specs=(P("tensor", "dp"), P("dp", "tensor"), P("dp", "tensor")),
        check_vma=False,
    )
```

```python
import math

import jax
import jax.numpy as jnp
import numpy as np
from jax import lax
from jax.experimental import pallas as pl
from jax.experimental.pallas import tpu as pltpu
from jax.sharding import PartitionSpec as P

MESH = pl.DeviceIdType.MESH
F32, BF16 = jnp.float32, jnp.bfloat16
B = 128
FL, DL = 1664, 1024
NZ, NT = 8, 16
HALF = 896
WIDTHS = (896, 768)
ROWS = NZ * B
STRIPS = ((0, 256), (256, 256), (512, 256), (768, B), (896, 256), (1152, 256), (1408, B), (1536, B))
ORDER = tuple((k, h) for k in range(6) for h in range(2)) + tuple((k, h) for h in range(2) for k in range(6, 8))
CHUNKS = ((0, 512), (512, 384), (896, 256), (1152, 256), (1408, B), (1536, B))
STRIPS_OF = ((0, 1), (2, 3), (4,), (5,), (6,), (7,))
RING = 4
TURNS = ((0, 0, 512), (1, 0, 256), (1, 512, 256))
PIECES = ((0, 0, 896), (1, 0, 512), (1, 512, 256))


def dot(a, b):
    return jnp.dot(a, b, preferred_element_type=F32)


def dot_t(a, b):
    return lax.dot_general(a, b, (((1,), (1,)), ((), ())), preferred_element_type=F32)


def block_rows(index, size=B):
    return pl.ds(pl.multiple_of(index * size, size), size)


def kernel(
    gate_hbm, up_hbm, codes_hbm, scales_hbm, grad_hbm, had_hbm,
    out_ref, grad_ref_out,
    gate_ref, up_ref, codes_v, scales_ref, grad_ref, had_ref,
    w_all, hid, mix_in, mix_out, acts, grads,
    cpart, crecv, csum, yrecv, xsend, xrecv, osend, oacc,
    back0, back1, back2, back3, ring0, ring1, ring2, ring3, back_last, direct, rot_grad, grad_hid,
    in_sem, w_s, w_r, a_s, a_r, e_s, e_r, ag_s, ag_r,
    gd_s, gd_r, gx_s, gx_r, gy_s, gy_r, gc_s, gc_r,
    c_s, c_r, y_s, y_r, x_s, x_r, o_s, o_r, rs_s, rs_r, ds_s, ds_r,
):
    d, t = lax.axis_index("dp"), lax.axis_index("tensor")
    back, ring = (back0, back1, back2, back3), (ring0, ring1, ring2, ring3)
    z, xl = lax.div(d, 2), lax.rem(d, 2)
    y, xh, core = lax.div(t, 4), lax.rem(lax.div(t, 2), 2), lax.rem(t, 2)

    def dev(z_=z, xl_=xl, y_=y, xh_=xh, c_=core):
        return (z_ * 2 + xl_, y_ * 4 + xh_ * 2 + c_)

    def zmod(v):
        return lax.rem(v + NZ, NZ)

    partner = dev(xl_=1 - xl)
    diagonal = dev(xl_=1 - xl, c_=1 - core)
    sibling = dev(c_=1 - core)
    across = dev(xh_=1 - xh)
    z_next = (dev(z_=zmod(z + 1)), dev(z_=zmod(z - 1)))
    y_peer = [dev(y_=lax.rem(y + r, 4)) for r in range(4)]
    sent = []

    def copy(src, dst, send, recv, device):
        return pltpu.make_async_remote_copy(
            src_ref=src, dst_ref=dst, send_sem=send, recv_sem=recv, device_id=device, device_id_type=MESH
        )

    def push(*args):
        op = copy(*args)
        op.start()
        sent.append(op)

    def arrived(dst, send, recv):
        copy(dst, dst, send, recv, sibling).wait_recv()

    first = pl.ds(0, STRIPS[0][1])
    rest = pl.ds(STRIPS[0][1], FL - STRIPS[0][1])
    fetches = [
        pltpu.make_async_copy(src, dst, in_sem.at[i])
        for i, (src, dst) in enumerate((
            (scales_hbm, scales_ref),
            (codes_hbm.at[first, :], codes_v.at[first, :]),
            (gate_hbm, gate_ref),
            (up_hbm, up_ref),
            (grad_hbm, grad_ref),
            (codes_hbm.at[rest, :], codes_v.at[rest, :]),
            (had_hbm, had_ref),
        ))
    ]
    for fetch in fetches:
        fetch.start()

    barrier = pltpu.get_barrier_semaphore()

    def greet(j, carry):
        pl.semaphore_signal(barrier, inc=1, device_id=(d, lax.rem(t + j, NT)), device_id_type=MESH)
        return carry

    lax.fori_loop(1, NT, greet, 0)
    z_peer = [dev(z_=lax.rem(z + j, NZ)) for j in range(NZ)]
    for device in (*z_peer[1:], partner, diagonal):
        pl.semaphore_signal(barrier, inc=1, device_id=device, device_id_type=MESH)

    def weight_piece(width, k, h):
        start, size = STRIPS[k]
        return w_all.at[width, pl.ds(start, size), pl.ds(h * 512, 512)]

    def weight_push(k, h):
        push(weight_piece(xl, k, h), weight_piece(xl, k, h), w_s.at[h, k], w_r.at[h, k], partner)

    def weight_arrived(k, h):
        arrived(weight_piece(1 - xl, k, h), w_s.at[h, k], w_r.at[h, k])

    def dequantize(k):
        start, size = STRIPS[k]
        for i in range(start // B, (start + size) // B):
            rows = slice(i * B, (i + 1) * B)
            for j in range(DL // B):
                cols = slice(j * B, (j + 1) * B)
                scale = jnp.broadcast_to(scales_ref[j : j + 1, i : i + 1], (B, B))
                w_all[xl, rows, cols] = (codes_v[rows, cols].astype(F32) * scale).astype(BF16)

    fetches[0].wait()
    fetches[1].wait()
    dequantize(0)
    fetches[2].wait()
    fetches[3].wait()

    def hidden_rows(i, carry):
        rows = block_rows(i, 16)
        gate = gate_ref[rows, :].astype(F32)
        value = (gate * jax.nn.sigmoid(gate) * up_ref[rows, :].astype(F32)).astype(BF16)
        hid[0, rows, :] = value[:, :HALF]
        hid[1, rows, : WIDTHS[1]] = value[:, HALF:]
        hid[1, rows, WIDTHS[1] :] = jnp.zeros((16, HALF - WIDTHS[1]), BF16)
        rot_grad[1, rows, WIDTHS[1] :] = jnp.zeros((16, HALF - WIDTHS[1]), BF16)
        return carry

    lax.fori_loop(0, 8, hidden_rows, 0)
    pl.semaphore_wait(barrier, NT - 1 + NZ - 1 + 2)

    def sixteen(p):
        return block_rows(lax.div(p, 2), 16)

    def peers(body):
        def step(j, carry):
            body(j)
            return carry

        lax.fori_loop(1, NT, step, 0)

    def peers_of(group, body):
        other = lax.rem(core + group, 2)

        def step(i, carry):
            body(2 * i + other)
            return carry

        lax.fori_loop(1 - other, NT // 2, step, 0)

    def mix(i, start, size):
        had = had_ref[...]
        for b in range(start // B, (start + size) // B):
            cols = slice(b * B, (b + 1) * B)
            mixed = dot(mix_in[i, :, :, cols].reshape(256, B), had)
            parts = [mixed[g * 16 : (g + 1) * 16] for g in range(NT)]
            for bit in (1, 2, 4, 8):
                parts = [parts[g] + parts[g ^ bit] if not g & bit else parts[g ^ bit] - parts[g] for g in range(NT)]
            for g in range(NT):
                mix_out[i, g, :, cols] = (parts[g] * (1.0 / math.sqrt(NT * B))).astype(BF16)

    def first_copy(j):
        p = lax.rem(t + j, NT)
        return copy(hid.at[lax.rem(p, 2), sixteen(p), :], mix_in.at[0, t], a_s.at[0, j], a_r.at[0, j], (d, p))

    def first_back(j):
        p = lax.rem(t + j, NT)
        landing = acts.at[core, block_rows(z * 8 + lax.div(t, 2), 16), :]
        return copy(mix_out.at[0, p], landing, a_s.at[1, j], a_r.at[1, j], (d, p))

    def first_scatter():
        peers(lambda j: first_copy(j).start())
        mix_in[0, t] = hid[core, sixteen(t), :]

    def first_mix():
        def came(j):
            arrived(mix_in.at[0, lax.rem(t - j + NT, NT)], a_s.at[0, j], a_r.at[0, j])

        peers(came)
        mix(0, 0, HALF)
        peers(lambda j: first_back(j).start())
        acts[core, block_rows(z * 8 + lax.div(t, 2), 16), :] = mix_out[0, t]

    def first_done():
        def came(j):
            p = lax.rem(t - j + NT, NT)
            landing = acts.at[lax.rem(p, 2), block_rows(z * 8 + lax.div(p, 2), 16), :]
            arrived(landing, a_s.at[1, j], a_r.at[1, j])

        peers(came)

    def last_copy(piece, j):
        group, start, size = PIECES[piece]
        p, cols = lax.rem(t + j, NT), pl.ds(start, size)
        src = rot_grad.at[group, sixteen(p), cols]
        return copy(src, mix_in.at[1, t, :, cols], e_s.at[0, piece, j], e_r.at[0, piece, j], (d, p))

    def last_back(piece, j):
        group, start, size = PIECES[piece]
        p, cols = lax.rem(t + j, NT), pl.ds(start, size)
        landing = grad_hid.at[group, sixteen(t), cols]
        return copy(mix_out.at[1, p, :, cols], landing, e_s.at[1, piece, j], e_r.at[1, piece, j], (d, p))

    def last_scatter(piece):
        group, start, size = PIECES[piece]
        peers_of(group, lambda j: last_copy(piece, j).start())

        @pl.when(core == group)
        def _():
            mix_in[1, t, :, start : start + size] = rot_grad[group, sixteen(t), start : start + size]

    def last_mix(piece):
        group, start, size = PIECES[piece]

        def came(j):
            landing = mix_in.at[1, lax.rem(t - j + NT, NT), :, pl.ds(start, size)]
            arrived(landing, e_s.at[0, piece, j], e_r.at[0, piece, j])

        @pl.when(core == group)
        def _():
            peers(came)
            mix(1, start, size)
            peers(lambda j: last_back(piece, j).start())
            grad_hid[group, sixteen(t), start : start + size] = mix_out[1, t, :, start : start + size]

    def last_done():
        for piece, (group, start, size) in enumerate(PIECES):

            def came(j):
                p = lax.rem(t - j + NT, NT)
                landing = grad_hid.at[group, sixteen(p), pl.ds(start, size)]
                arrived(landing, e_s.at[1, piece, j], e_r.at[1, piece, j])

            peers_of(group, came)

    def drain():
        peers(lambda j: first_copy(j).wait_send())
        peers(lambda j: first_back(j).wait_send())
        for piece, (group, _, _) in enumerate(PIECES):
            peers_of(group, lambda j: last_copy(piece, j).wait_send())

            @pl.when(core == group)
            def _():
                peers(lambda j: last_back(piece, j).wait_send())

    own_rows, across_rows = block_rows(2 * y + xh), block_rows(2 * y + 1 - xh)
    diagonal_copy = copy(grad_ref, grads.at[xl, own_rows, :], gd_s, gd_r, diagonal)

    def grad_own():
        @pl.when(core != xl)
        def _():
            arrived(grads.at[core, own_rows, :], gd_s, gd_r)

        mine = grads.at[core, own_rows, :]
        push(mine, mine, gx_s, gx_r, across)
        for r in (1, 3, 2):
            push(mine, mine, gy_s.at[0, r], gy_r.at[0, r], y_peer[r])
        push(mine, mine, gc_s.at[0, 0], gc_r.at[0, 0], sibling)

    def grad_across():
        piece = grads.at[core, across_rows, :]
        arrived(piece, gx_s, gx_r)
        for r in (1, 3, 2):
            push(piece, piece, gy_s.at[1, r], gy_r.at[1, r], y_peer[r])
        push(piece, piece, gc_s.at[1, 0], gc_r.at[1, 0], sibling)

    def grad_y(f, r):
        source = lax.rem(y - r + 4, 4)
        piece = grads.at[core, block_rows(2 * source + (1 - xh if f else xh)), :]
        arrived(piece, gy_s.at[f, r], gy_r.at[f, r])
        push(piece, piece, gc_s.at[f, r], gc_r.at[f, r], sibling)

    def grad_done():
        for f in range(2):
            for r in range(4):
                source = lax.rem(y - r + 4, 4)
                piece = grads.at[1 - core, block_rows(2 * source + (1 - xh if f else xh)), :]
                arrived(piece, gc_s.at[f, r], gc_r.at[f, r])

    def ag_copy(way, s, group):
        block = zmod(z - s) if way == 0 else zmod(z + s)
        piece = acts.at[group, block_rows(block), pl.ds(0, WIDTHS[group])]
        return (piece, piece, ag_s.at[way, s, group], ag_r.at[way, s, group], z_next[way])

    def ag_step(s):
        for group in range(2):
            for way in range(2):
                if s and (s < 4 or way == group):
                    block = zmod(z - s) if way == 0 else zmod(z + s)
                    piece = acts.at[group, block_rows(block), pl.ds(0, WIDTHS[group])]
                    arrived(piece, ag_s.at[way, s - 1, group], ag_r.at[way, s - 1, group])
                if s < 3 or (s == 3 and way == group):
                    push(*ag_copy(way, s, group))

    def rs_push(way, k, s):
        block = zmod(z + 4 - s) if way == 0 else zmod(z - 4 + s)
        if s == 0:
            piece = back[k].at[block_rows(2 * block + way, 64), :]
            landing = ring[k].at[way, 0, pl.ds(0, 64), :]
        else:
            piece = back[k].at[block_rows(block), :]
            landing = ring[k].at[way, s]
        push(piece, landing, rs_s.at[way, k, s], rs_r.at[way, k, s], z_next[way])

    def rs_arrived(way, k, s):
        landing = ring[k].at[way, s, pl.ds(0, B if s else 64), :]
        arrived(landing, rs_s.at[way, k, s], rs_r.at[way, k, s])

    def product(k, h):
        start, size = CHUNKS[k]
        units = slice(start, start + size)
        for strip in STRIPS_OF[k]:
            for part in (0, 1) if h is None else (h,):
                weight_arrived(strip, part)

        def one(m, carry):
            rows = block_rows(m, 256)
            if h == 1:
                term = back[k][rows, :] if k < RING else back_last[k - RING, rows, :]
                term = term.astype(F32) + dot_t(grads[1 - xl, rows, 512:], w_all[1 - xl, units, 512:])
            else:
                seen = slice(0, 512 if h == 0 else DL)
                term = dot_t(grads[xl, rows, :], w_all[xl, units, :])
                term = term + dot_t(grads[1 - xl, rows, seen], w_all[1 - xl, units, seen])
            if k < RING:
                back[k][rows, :] = term.astype(BF16)
            else:
                back_last[k - RING, rows, :] = term.astype(BF16)
            return carry

        lax.fori_loop(0, ROWS // 256, one, 0)

    def back_total(k, arrivals):
        start, size = CHUNKS[k]
        mine = back[k][block_rows(z), :] if k < RING else back_last[k - RING, block_rows(z), :]
        total = mine.astype(F32)
        for came in arrivals:
            total = total + came.astype(F32)
        total = total.astype(BF16)
        for b in range(size // B):
            group, place = divmod(start // B + b, HALF // B)
            rot_grad[group, :, place * B : (place + 1) * B] = total[:, b * B : (b + 1) * B]

    def back_step(k, s):
        if s == 0:
            product(k, None)
            for way in range(2):
                rs_push(way, k, 0)
        elif s < 4:
            for way in range(2):
                rs_arrived(way, k, s - 1)
                block = zmod(z + 4 - s) if way == 0 else zmod(z - 4 + s)
                if s == 1:
                    rows = block_rows(2 * block + way, 64)
                    came = ring[k][way, 0, :64, :]
                else:
                    rows = block_rows(block)
                    came = ring[k][way, s - 1]
                back[k][rows, :] = (back[k][rows, :].astype(F32) + came.astype(F32)).astype(BF16)
                rs_push(way, k, s)
        else:
            for way in range(2):
                rs_arrived(way, k, 3)
            back_total(k, [ring[k][way, 3] for way in range(2)])

    def direct_step(k, s):
        i = k - RING
        if s == 0:
            product(k, 1)
            for j in (4, 3, 5, 2, 6, 1, 7):
                piece = back_last.at[i, block_rows(zmod(z + j)), :]
                push(piece, direct.at[i, j - 1], ds_s.at[i, j], ds_r.at[i, j], z_peer[j])
        else:
            for j in range(1, NZ):
                arrived(direct.at[i, j - 1], ds_s.at[i, j], ds_r.at[i, j])
            back_total(k, [direct[i, j - 1] for j in range(1, NZ)])

    def out_rows(r):
        return block_rows(lax.rem(y + r, 4), 256)

    def out_product(turn, r):
        late, start, size = TURNS[turn]
        width = 1 - xl if late else xl
        rows, share = out_rows(r), pl.ds(0, size)
        for h in range(2):
            cols = slice(start + h * size, start + (h + 1) * size)
            term = dot(acts[0, rows, :], w_all[width, :HALF, cols])
            term = term + dot(acts[1, rows, : WIDTHS[1]], w_all[width, HALF:, cols])
            cpart[turn, h, rows, :size] = term.astype(BF16)
        landing = crecv.at[turn, rows, share]
        push(cpart.at[turn, 1 - core, rows, share], landing, c_s.at[turn, r], c_r.at[turn, r], sibling)

    def out_core_sum(turn, r):
        size = TURNS[turn][2]
        rows, share = out_rows(r), pl.ds(0, size)
        arrived(crecv.at[turn, rows, share], c_s.at[turn, r], c_r.at[turn, r])
        total = cpart[turn, core, rows, :size].astype(F32) + crecv[turn, rows, :size].astype(F32)
        csum[turn, rows, :size] = total.astype(BF16)
        if r:
            landing = yrecv.at[turn, r - 1, :, share]
            push(csum.at[turn, rows, share], landing, y_s.at[turn, r], y_r.at[turn, r], y_peer[r])

    def out_y_part(turn, side):
        size = TURNS[turn][2]
        total = csum[turn, block_rows(2 * y + side), :size].astype(F32)
        for r in range(3):
            total = total + yrecv[turn, r, block_rows(side), :size].astype(F32)
        return total

    def out_y_sum(turn):
        size = TURNS[turn][2]
        share = pl.ds(0, size)
        for r in range(1, 4):
            arrived(yrecv.at[turn, r - 1, :, share], y_s.at[turn, r], y_r.at[turn, r])
        xsend[turn, :, :size] = out_y_part(turn, 1 - xh).astype(BF16)
        push(xsend.at[turn, :, share], xrecv.at[turn, :, share], x_s.at[turn], x_r.at[turn], across)

    def out_cols(turn, sender):
        _, start, size = TURNS[turn]
        return pl.ds(pl.multiple_of(start + sender * size, 256), size)

    def out_copy(turn):
        device = dev(xl_=1 - xl, c_=xl) if turn else sibling
        share = pl.ds(0, TURNS[turn][2])
        return copy(osend.at[turn, :, share], oacc.at[:, out_cols(turn, core)], o_s.at[turn], o_r.at[turn, core], device)

    def out_place(turn):
        size = TURNS[turn][2]
        arrived(xrecv.at[turn, :, pl.ds(0, size)], x_s.at[turn], x_r.at[turn])
        osend[turn, :, :size] = (out_y_part(turn, xh) + xrecv[turn, :, :size].astype(F32)).astype(BF16)
        if turn == 0:

            @pl.when(core == xl)
            def _():
                oacc[:, out_cols(0, core)] = osend[0]

            @pl.when(core != xl)
            def _():
                out_copy(0).start()
        else:
            out_copy(turn).start()

    def out_done():
        @pl.when(core == xl)
        def _():
            arrived(oacc.at[:, out_cols(0, 1 - core)], o_s.at[0], o_r.at[0, 1 - core])

        @pl.when(core != xl)
        def _():
            for turn in (1, 2):
                for sender in range(2):
                    arrived(oacc.at[:, out_cols(turn, sender)], o_s.at[turn], o_r.at[turn, sender])

    first_scatter()
    fetches[4].wait()

    @pl.when(core != xl)
    def _():
        diagonal_copy.start()

    @pl.when(core == xl)
    def _():
        grads[core, own_rows, :] = grad_ref[...]

    weight_push(0, 0)
    fetches[5].wait()
    for k in range(1, len(STRIPS)):
        dequantize(k)
    fetches[6].wait()
    first_mix()
    grad_own()
    for k, h in ORDER[1:]:
        weight_push(k, h)
    first_done()
    ag_step(0)
    grad_across()
    for r in (1, 3, 2):
        grad_y(0, r)
    ag_step(1)
    for r in (1, 3, 2):
        grad_y(1, r)
    grad_done()

    starts = (0, 2, 4, 6)

    def tick(i):
        for s in (4, 3, 2, 1, 0):
            if i - s in starts:
                back_step(starts.index(i - s), s)

    tick(0)
    ag_step(2)
    tick(1)
    ag_step(3)
    tick(2)
    ag_step(4)
    tick(3)
    out_product(0, 1)
    out_product(0, 2)
    tick(4)
    out_product(0, 3)
    out_product(0, 0)
    out_core_sum(0, 1)
    out_core_sum(0, 2)
    tick(5)
    out_core_sum(0, 3)
    out_core_sum(0, 0)
    tick(6)
    last_scatter(0)
    for k in (4, 5):
        product(k, 0)
    tick(7)
    for r in (1, 2, 3, 0):
        out_product(1, r)
    direct_step(4, 0)
    tick(8)
    for r in (1, 2, 3, 0):
        out_core_sum(1, r)
    direct_step(5, 0)
    out_y_sum(0)
    for r in (1, 2, 3, 0):
        out_product(2, r)
    tick(9)
    for r in (1, 2, 3, 0):
        out_core_sum(2, r)
    last_mix(0)
    tick(10)
    last_scatter(1)
    out_y_sum(1)
    out_place(0)
    direct_step(4, 1)
    direct_step(5, 1)
    last_scatter(2)
    out_place(1)
    out_y_sum(2)
    last_mix(1)
    last_mix(2)
    out_place(2)
    out_done()
    last_done()
    out_ref[...] = oacc[...]
    grad_ref_out[:, :HALF] = grad_hid[0]
    grad_ref_out[:, HALF:] = grad_hid[1, :, : WIDTHS[1]]

    for op in sent:
        op.wait_send()

    @pl.when(core != xl)
    def _():
        diagonal_copy.wait_send()
        out_copy(0).wait_send()

    out_copy(1).wait_send()
    out_copy(2).wait_send()
    drain()


def finish(gate_ref, up_ref, grad_ref, sums_ref, out_ref, gate_grad_ref, up_grad_ref):
    def some_rows(i, carry):
        rows = block_rows(i, 16)
        gate, up = gate_ref[rows, :].astype(F32), up_ref[rows, :].astype(F32)
        grad = grad_ref[rows, :].astype(F32)
        sig = jax.nn.sigmoid(gate)
        up_grad_ref[rows, :] = (grad * (gate * sig)).astype(BF16)
        gate_grad_ref[rows, :] = (grad * up * sig * (1.0 + gate * (1.0 - sig))).astype(BF16)
        return carry

    lax.fori_loop(0, B // 16, some_rows, 0)
    out_ref[...] = sums_ref[...]


def hadamard():
    index = np.arange(B)
    bits = index[:, None] & index[None, :]
    parity = sum(bits >> s & 1 for s in range(7)) % 2
    return (1 - 2 * parity).astype(np.float32)


def on_device(gate_act, up_act, down_codes, down_scales, grad_out):
    vmem, dma = pltpu.VMEM, pltpu.SemaphoreType.DMA
    whole = pl.BlockSpec(memory_space=pltpu.VMEM)
    layer_output, grad_hidden = pl.pallas_call(
        kernel,
        out_shape=(jax.ShapeDtypeStruct((B, DL), BF16), jax.ShapeDtypeStruct((B, FL), BF16)),
        in_specs=[pl.BlockSpec(memory_space=pl.ANY)] * 6,
        out_specs=(whole, whole),
        scratch_shapes=[
            vmem((B, FL), BF16),
            vmem((B, FL), BF16),
            vmem((FL, DL), BF16),
            vmem((DL // B, FL // B), F32),
            vmem((B, DL), BF16),
            vmem((B, B), BF16),
            vmem((2, FL, DL), BF16),
            vmem((2, B, HALF), BF16),
            vmem((2, NT, 16, HALF), BF16),
            vmem((2, NT, 16, HALF), BF16),
            vmem((2, ROWS, HALF), BF16),
            vmem((2, ROWS, DL), BF16),
            vmem((3, 2, ROWS, 512), BF16),
            vmem((3, ROWS, 512), BF16),
            vmem((3, ROWS, 512), BF16),
            vmem((3, 3, 256, 512), BF16),
            vmem((3, B, 512), BF16),
            vmem((3, B, 512), BF16),
            vmem((3, B, 512), BF16),
            vmem((B, DL), BF16),
            *(vmem((ROWS, size), BF16) for _, size in CHUNKS[:RING]),
            *(vmem((2, 4, B, size), BF16) for _, size in CHUNKS[:RING]),
            vmem((len(CHUNKS) - RING, ROWS, B), BF16),
            vmem((len(CHUNKS) - RING, NZ - 1, B, B), BF16),
            vmem((2, B, HALF), BF16),
            vmem((2, B, HALF), BF16),
            dma((7,)),
            dma((2, len(STRIPS))), dma((2, len(STRIPS))),
            dma((2, NT)), dma((2, NT)),
            dma((2, 3, NT)), dma((2, 3, NT)),
            dma((2, 4, 2)), dma((2, 4, 2)),
            dma, dma,
            dma, dma,
            dma((2, 4)), dma((2, 4)),
            dma((2, 4)), dma((2, 4)),
            dma((3, 4)), dma((3, 4)),
            dma((3, 4)), dma((3, 4)),
            dma((3,)), dma((3,)),
            dma((3,)), dma((3, 2)),
            dma((2, RING, 4)), dma((2, RING, 4)),
            dma((2, NZ)), dma((2, NZ)),
        ],
        compiler_params=pltpu.CompilerParams(
            collective_id=0, has_side_effects=True, vmem_limit_bytes=56 * 1024 * 1024
        ),
    )(gate_act, up_act, down_codes, down_scales.T, grad_out, jnp.asarray(hadamard(), BF16))
    layer_output, gate_grad, up_grad = pl.pallas_call(
        finish,
        out_shape=(
            jax.ShapeDtypeStruct((B, DL), BF16),
            jax.ShapeDtypeStruct((B, FL), BF16),
            jax.ShapeDtypeStruct((B, FL), BF16),
        ),
        in_specs=[whole] * 4,
        out_specs=(whole,) * 3,
    )(gate_act, up_act, grad_hidden, layer_output)
    return (layer_output, gate_grad, up_grad)


def solution(mesh):
    return jax.shard_map(
        on_device,
        mesh=mesh,
        in_specs=(
            P("dp", "tensor"),
            P("dp", "tensor"),
            P("tensor", "dp"),
            P("tensor", "dp"),
            P("tensor", "dp"),
        ),
        out_specs=(P("tensor", "dp"), P("dp", "tensor"), P("dp", "tensor")),
        check_vma=False,
    )
```
